256 devices in a mesh: row: 8 (over y, core), leaf: 32 (over x, z).
Axes of the slice: x: 4, y: 4, z: 8, core: 2. Of those that a mesh axis runs over, the one named last changes fastest.
Arguments:
- diag_blocks: float32 [32, 24, 256, 256], P('leaf', 'row'), as said below
- panel: float32 [32, 24, 768, 256], P('leaf', None, 'row'), may hold values from -1.5 to 1.5
- parent: int32 [32, 24, 1], replicated, may hold values from 0 to 31; in each aligned block of 24 rows (0 to 23, 24 to 47, ..., all dimensions but the last counted through in order) at most 2 rows name the same one
- rel: int32 [32, 24, 6], replicated, may hold values from 0 to 7, as said below
- front: float32 [32, 1024, 1024], P('leaf', None, 'row'), may hold values from -6 to 6
Outputs:
- factor_diag: float32 [32, 24, 256, 256], P('leaf', 'row')
- factor_panel: bfloat16 [32, 24, 768, 256], P('leaf', None, 'row')
- new_front: float32 [32, 1024, 1024], P('leaf', None, 'row')
The draws below stay inside these ranges and needn't reach their ends.
Inputs may be any that keep to these rules, and one draw needn't show every extreme that they name: Among the 24 supernodes of one leaf index at most 2 have the same parent owner, and some leaf index reaches 2. `rel`: the 6 entries of each supernode name different blocks of the parent's front, in rising order. `diag_blocks`: every block is symmetric positive definite.
All inputs are finite; a program needn't handle non-finite values.
Results may differ from the reference program's by a relative error of at most 0.0011.
Values may be sent and summed in bfloat16 or wider, within the bound.
No kernel may reach another device: no remote copies, remote signals or barrier semaphores. Data moves between devices by JAX's collectives and lax.ppermute only.
A program may use at most 128 MiB of HBM per device.

```python
import math
import jax
import jax.numpy as jnp
import numpy as np
from jax import lax

W = 256
BS = 128
FB = 8
P_SIZE = 6
K = 24
MOST = 2
F = 1024
N_LEAF = 32


def draw_diag_blocks(key, part):
    first_key, second_key = jax.random.split(jax.random.fold_in(key, 11), 2)
    raw = jax.random.normal(first_key, (N_LEAF, K, W, W), jnp.float32)
    raw = jnp.clip(raw, -6.0, 6.0)
    symmetric = (raw + jnp.swapaxes(raw, -1, -2)) * (0.7071 / W ** 0.5)
    shifts = jax.random.uniform(second_key, (N_LEAF, K, W), jnp.float32, 2.4, 3.2)
    identity = jnp.eye(W, dtype=jnp.float32)
    places = jnp.arange(W, dtype=jnp.int32)
    distance = jnp.abs(places[:, None] - places[None, :]).astype(jnp.float32)
    kernel = 0.3 * jnp.exp(-distance / 8.0)
    matrix = symmetric + identity * shifts[..., None] + kernel
    return matrix.astype(jnp.float32)


def draw_rel(key, part):
    scores = jax.random.randint(jax.random.fold_in(key, 23), (N_LEAF, K, FB), 0, 1 << 20)
    scores = scores * FB + jnp.arange(FB, dtype=jnp.int32)
    chosen = jnp.argsort(scores, axis=-1)[..., :P_SIZE]
    return jnp.sort(chosen, axis=-1).astype(jnp.int32)


def shard_levels(key, extent, shards, smallest, largest):
    factor_of = 1.0
    for axis_at, parts in shards:
        heights = jax.random.uniform(jax.random.fold_in(jax.random.fold_in(key, 6), axis_at), (parts,), jnp.float32, smallest / len(shards), largest / len(shards))
        factor_of = factor_of * jnp.repeat(jnp.exp(heights), extent[axis_at] // parts).reshape((-1,) + (1,) * (len(extent) - 1 - axis_at))
    return factor_of


def shared_out(own_key, own, number, rows, amount, top, limit, lean):
    order = jax.random.permutation(own_key, amount)
    crowded, common = shares(amount, rows * top, limit, lean, True), shares(amount, rows * top, limit, lean, False)
    places = jnp.arange(amount)

    def named(sizes, turn):
        used = int((sizes > 0).sum())
        fixed = max(1, used // 4)
        passed = fixed + (places - fixed + turn * (used - fixed)) % max(1, amount - fixed)
        return jnp.zeros((amount,), jnp.int32).at[order[jnp.where(places < fixed, places, passed)]].set(jnp.asarray(sizes, jnp.int32))

    sizes = jnp.where(number % 4 == 0, named(crowded, number // 4), named(common, number - number // 4 - 1))
    mixed = jax.random.permutation(jax.random.fold_in(own, 3), amount)
    source_of, sink = mixed[0:amount // 2 * 2:2], mixed[1:amount // 2 * 2:2]
    margin = jnp.minimum(sizes[source_of] - 1, limit - sizes[sink]) // 2
    margin = jnp.where((source_of == order[0]) | (sink == order[0]) | (sizes[sink] == 0), 0, jnp.maximum(margin, 0))
    passed = jax.random.randint(jax.random.fold_in(own, 4), (amount // 2,), 0, 1 << 20) % (margin + 1)
    sizes = sizes.at[source_of].add(-passed).at[sink].add(passed)
    labels = jnp.searchsorted(jnp.cumsum(sizes), jnp.arange(rows * top), side="right").astype(jnp.int32)
    table = labels.reshape(top, rows).T
    table = table[jax.random.permutation(jax.random.fold_in(own, 1), rows)]
    turn = jax.random.randint(jax.random.fold_in(own, 2), (rows, 1), 0, top)
    return jnp.take_along_axis(table, (jnp.arange(top)[None, :] + turn) % top, axis=1)


def shares(amount, total, limit, slope, full):
    weights = [(1 << 20) // math.isqrt(rank ** slope) + 1 for rank in range(1, amount + 1)]
    largest = limit if full else min(limit, max(-(-total // amount), total * weights[0] // sum(weights)))
    least = 1 if total - largest >= amount - 1 else 0
    holding, rest = [largest] + [least] * (amount - 1), total - largest - least * (amount - 1)
    while rest > 0:
        candidates = [i for i in range(1, amount) if holding[i] < largest] or [i for i in range(1, amount) if holding[i] < limit]
        mass, left = sum([weights[i] for i in candidates]), rest
        for i in candidates:
            more = min(limit - holding[i], max(1, left * weights[i] // mass), rest)
            holding[i] = holding[i] + more
            rest = rest - more
    return np.array(holding)


def noise(stream_key, extent, scale, bound, cuts=(), kind=jnp.bfloat16):
    loudness = shard_levels(stream_key, extent, cuts, -0.22, 0.18) if cuts else 1.0
    array = jax.random.normal(stream_key, extent, jnp.float32) * scale * loudness
    return jnp.minimum(jnp.maximum(array, -bound), bound).astype(kind)


def setup_inputs(seed: int = 0) -> dict:
    splits = jax.random.split(jax.random.key(seed), 6)
    diag_blocks = draw_diag_blocks(jax.random.fold_in(splits[5], 71), 0)
    panel = noise(splits[1], (N_LEAF, K, P_SIZE * BS, W), 0.25, 1.5, ((0, 32), (2, 8)), jnp.float32)
    parent_keys = jax.random.split(jax.random.fold_in(splits[2], 1), N_LEAF * K // K)
    parent_turns = jax.random.permutation(jax.random.fold_in(splits[2], 3), N_LEAF * K // K)
    parent = jax.vmap(lambda own, number: shared_out(jax.random.fold_in(splits[2], 2), own, number, K, N_LEAF, 1, MOST, 2))(parent_keys, parent_turns).reshape((N_LEAF, K, 1))
    rel = draw_rel(jax.random.fold_in(splits[5], 71), 0)
    front = noise(splits[4], (N_LEAF, F, F), 1.0, 6.0, ((0, 32), (2, 8)), jnp.float32)
    return dict(diag_blocks=diag_blocks, panel=panel, parent=parent, rel=rel, front=front)


def reference(diag_blocks, panel, parent, rel, front):
    factor_diag = jnp.linalg.cholesky(diag_blocks)
    solved = jax.scipy.linalg.solve_triangular(factor_diag, jnp.swapaxes(panel, -1, -2), lower=True)
    factor_panel = jnp.swapaxes(solved, -1, -2).astype(jnp.bfloat16)
    flat_panels = factor_panel.reshape(N_LEAF * K, P_SIZE * BS, W)
    flat_parent = parent.reshape(N_LEAF * K).astype(jnp.int32)
    flat_rel = rel.reshape(N_LEAF * K, P_SIZE).astype(jnp.int32)
    offsets = jnp.arange(BS, dtype=jnp.int32)

    def add_child(fronts, child_data):
        child_panel, owner_id, blocks = child_data
        schur = jnp.dot(child_panel.astype(jnp.float32), child_panel.T.astype(jnp.float32), preferred_element_type=jnp.float32).astype(jnp.bfloat16)
        schur = lax.optimization_barrier(schur).astype(jnp.float32)
        row_ids = (blocks[:, None] * BS + offsets[None, :]).reshape(-1).astype(jnp.int32)
        fronts = fronts.at[owner_id, row_ids[:, None], row_ids[None, :]].add(-schur)
        return (fronts, None)
    new_front, _ = lax.scan(add_child, front, (flat_panels, flat_parent, flat_rel))
    return (factor_diag, factor_panel, new_front)
```

```python
import functools

import jax
import jax.numpy as jnp
from jax import lax
from jax.experimental import pallas as pl
from jax.experimental.pallas import tpu as pltpu
from jax.sharding import PartitionSpec as P

W = 256
BS = 128
FB = 8
P_SIZE = 6
K = 24
LEAVES = 32
ROWS = 8
OWN = K // ROWS
PANEL = P_SIZE * BS
PART = PANEL // ROWS
SLICE = W // ROWS
MOST = 2
SLOTS = LEAVES * MOST
NB = 64
HI = lax.Precision.HIGHEST
F32 = jnp.float32
BF16 = jnp.bfloat16

ANY = pl.BlockSpec(memory_space=pl.ANY)
VMEM = pl.BlockSpec(memory_space=pltpu.VMEM)
SMEM = pl.BlockSpec(memory_space=pltpu.SMEM)
PARAMS = pltpu.CompilerParams(vmem_limit_bytes=56 * 2**20)


def mm(a, b, trans_b=False):
    dims = (((1,), (1 if trans_b else 0,)), ((), ()))
    return lax.dot_general(a, b, dims, precision=HI, preferred_element_type=F32)


def eliminate(tiles, offset, nb):
    sub = lax.broadcasted_iota(jnp.int32, (8, 128), 0)
    for j in range(nb):
        first, jj = divmod(j, 8)
        lane = slice(offset + j, offset + j + 1)
        for ts in tiles:
            row = jnp.broadcast_to(ts[first][jj : jj + 1, :], (8, 128))
            pivot = jnp.broadcast_to(ts[first][jj : jj + 1, lane], (8, 128))
            scaled = row * (1.0 / pivot)
            for t in range(first, nb // 8):
                if t == first and jj == 7:
                    continue
                col = jnp.broadcast_to(ts[t][:, lane], (8, 128))
                if t == first:
                    col = jnp.where(sub > jj, col, 0.0)
                ts[t] = ts[t] - col * scaled
    return tiles


def factor_kernel(a_ref, l_ref, v_ref, s_ref):
    n, w = a_ref.shape[0], a_ref.shape[1]
    s_ref[...] = a_ref[...]
    lane = lax.broadcasted_iota(jnp.int32, (NB, 128), 1)
    sub = lax.broadcasted_iota(jnp.int32, (NB, 128), 0)
    for k in range(w // NB):
        lo, hi = k * NB, (k + 1) * NB
        off = lo % 128
        other = NB - off
        tile = slice(lo - off, lo - off + 128)
        own = (lane >= off) & (lane < off + NB)
        eye = (lane - other == sub).astype(F32)
        tiles = []
        for m in range(n):
            b = jnp.where(own, s_ref[m, lo:hi, tile], eye)
            tiles.append([b[8 * t : 8 * t + 8] for t in range(NB // 8)])
        tiles = eliminate(tiles, off, NB)
        for m in range(n):
            b = jnp.concatenate(tiles[m], axis=0)
            d = jnp.sum(jnp.where(lane - off == sub, b, 0.0), axis=1, keepdims=True)
            b = b * (1.0 / jnp.sqrt(d))
            up, inv = b[:, off : off + NB], b[:, other : other + NB]
            up = jnp.where(lane[:, :NB] >= sub[:, :NB], up, 0.0)
            inv = jnp.where(lane[:, :NB] <= sub[:, :NB], inv, 0.0)
            g = mm(inv, s_ref[m, lo:hi, :])
            left = [g[:, :lo]] if k else []
            right = [g[:, hi:]] if hi < w else []
            r = jnp.concatenate(left + [inv] + right, axis=1)
            col = lax.broadcasted_iota(jnp.int32, (NB, w), 1)
            v_ref[m, lo:hi, :] = jnp.where(col < hi, r, 0.0)
            zero = [jnp.zeros((NB, lo), F32)] if k else []
            ut = jnp.concatenate(zero + [up] + right, axis=1).T
            l_ref[m, :, lo:hi] = ut
            if hi < w:
                rest = s_ref[m, hi:, :]
                at = lax.broadcasted_iota(jnp.int32, rest.shape, 1)
                rest = jnp.where((at >= lo) & (at < hi), 0.0, rest)
                s_ref[m, hi:, :] = rest - mm(ut[hi:, :], r)


def factor(a):
    shape = jax.ShapeDtypeStruct(a.shape, F32)
    return pl.pallas_call(
        factor_kernel,
        out_shape=(shape, shape),
        in_specs=[VMEM],
        out_specs=(VMEM, VMEM),
        scratch_shapes=[pltpu.VMEM(a.shape, F32)],
        compiler_params=PARAMS,
        name="factor",
    )(a)


def split_kernel(r_ref, panel_ref, *refs):
    outs, sems = refs[:-1], refs[-1]
    copies = []
    for s in range(ROWS):
        to = lax.rem(r_ref[0] + s, ROWS)
        copies.append(
            pltpu.make_async_copy(panel_ref.at[pl.ds(to * OWN, OWN)], outs[s], sems.at[s])
        )
    for c in copies:
        c.start()
    for c in copies:
        c.wait()


def split(r, panel):
    piece = jax.ShapeDtypeStruct((OWN, PART, W), panel.dtype)
    return pl.pallas_call(
        split_kernel,
        out_shape=(piece,) * ROWS,
        in_specs=[SMEM, ANY],
        out_specs=(ANY,) * ROWS,
        scratch_shapes=[pltpu.SemaphoreType.DMA((ROWS,))],
        name="split",
    )(r, panel)


def join_kernel(r_ref, *refs):
    pieces, out_ref, sems = refs[:ROWS], refs[ROWS], refs[ROWS + 1]
    copies = []
    for s in range(ROWS):
        source = lax.rem(r_ref[0] + ROWS - s, ROWS)
        copies.append(
            pltpu.make_async_copy(pieces[s], out_ref.at[pl.ds(source * OWN, OWN)], sems.at[s])
        )
    for c in copies:
        c.start()
    for c in copies:
        c.wait()


def join(r, pieces):
    return pl.pallas_call(
        join_kernel,
        out_shape=jax.ShapeDtypeStruct((K,) + pieces[0].shape[1:], pieces[0].dtype),
        in_specs=[SMEM] + [ANY] * ROWS,
        out_specs=ANY,
        scratch_shapes=[pltpu.SemaphoreType.DMA((ROWS,))],
        name="join",
    )(r, *pieces)


def solve_kernel(r_ref, v_ref, *refs):
    pieces, xs, ts = refs[:ROWS], refs[ROWS : 2 * ROWS], refs[2 * ROWS : 3 * ROWS]
    p_ref, x_ref, t_ref, sems = refs[3 * ROWS :]
    r = r_ref[0]
    copies = []
    for s in range(ROWS):
        source = lax.rem(r + ROWS - s, ROWS)
        at = pl.ds(pl.multiple_of(source * PART, PART), PART)
        copies.append(pltpu.make_async_copy(pieces[s], p_ref.at[:, at], sems.at[s]))
    for c in copies:
        c.start()
    for c in copies:
        c.wait()
    one = lax.broadcasted_iota(jnp.int32, (W, W), 0) == lax.broadcasted_iota(jnp.int32, (W, W), 1)
    eye = one.astype(BF16)
    for m in range(OWN):
        x = mm(p_ref[m], v_ref[m], trans_b=True).astype(BF16)
        x_ref[m] = x
        t_ref[m] = lax.dot_general(
            eye, x, (((1,), (1,)), ((), ())), preferred_element_type=F32
        ).astype(BF16)
    for s in range(ROWS):
        to = lax.rem(r + s, ROWS)
        xs[s][...] = x_ref[:, pl.ds(pl.multiple_of(to * PART, PART), PART), :]
        ts[s][...] = t_ref[:, pl.ds(pl.multiple_of(to * SLICE, SLICE), SLICE), :]


def solve(r, inverse, pieces):
    row_piece = jax.ShapeDtypeStruct((OWN, PART, W), BF16)
    column_piece = jax.ShapeDtypeStruct((OWN, SLICE, PANEL), BF16)
    return pl.pallas_call(
        solve_kernel,
        out_shape=(row_piece,) * ROWS + (column_piece,) * ROWS,
        in_specs=[SMEM, VMEM] + [ANY] * ROWS,
        out_specs=(VMEM,) * (2 * ROWS),
        scratch_shapes=[
            pltpu.VMEM((OWN, PANEL, W), F32),
            pltpu.VMEM((OWN, PANEL, W), BF16),
            pltpu.VMEM((OWN, W, PANEL), BF16),
            pltpu.SemaphoreType.DMA((ROWS,)),
        ],
        compiler_params=PARAMS,
        name="solve",
    )(r, inverse, *pieces)


def outgoing_kernel(r_ref, owner_ref, *refs):
    pieces, out_ref = refs[:ROWS], refs[ROWS]
    used, place, sems = refs[ROWS + 1 :]
    for a in range(LEAVES):
        used[a] = 0
    for k in range(K):
        a = owner_ref[k]
        place[k] = MOST * a + used[a]
        used[a] = used[a] + 1
    copies = []
    for s in range(ROWS):
        source = lax.rem(r_ref[0] + ROWS - s, ROWS)
        for i in range(OWN):
            copies.append(
                pltpu.make_async_copy(
                    pieces[s].at[i], out_ref.at[place[source * OWN + i]], sems.at[s, i]
                )
            )
            copies[-1].start()
    for c in copies:
        c.wait()


def outgoing(r, owners, pieces):
    return pl.pallas_call(
        outgoing_kernel,
        out_shape=jax.ShapeDtypeStruct((SLOTS, SLICE, PANEL), BF16),
        in_specs=[SMEM, SMEM] + [ANY] * ROWS,
        out_specs=ANY,
        scratch_shapes=[
            pltpu.SMEM((LEAVES,), jnp.int32),
            pltpu.SMEM((K,), jnp.int32),
            pltpu.SemaphoreType.DMA((ROWS, OWN)),
        ],
        name="outgoing",
    )(r, owners, *pieces)


def children_kernel(leaf_ref, owner_ref, rel_ref, count_ref, slot_ref, block_ref):
    me = leaf_ref[0]

    def of_leaf(j, total):
        def of_node(k, carry):
            total, here = carry
            hit = owner_ref[j * K + k] == me

            @pl.when(hit)
            def _():
                slot_ref[total] = MOST * j + here
                for p in range(P_SIZE):
                    block_ref[total * P_SIZE + p] = rel_ref[(j * K + k) * P_SIZE + p]

            step = hit.astype(jnp.int32)
            return total + step, here + step

        return lax.fori_loop(0, K, of_node, (total, 0))[0]

    count_ref[0] = lax.fori_loop(0, LEAVES, of_leaf, 0)


def children(leaf, owners, rel):
    ints = lambda n: jax.ShapeDtypeStruct((n,), jnp.int32)
    return pl.pallas_call(
        children_kernel,
        out_shape=(ints(1), ints(SLOTS), ints(SLOTS * P_SIZE)),
        in_specs=[SMEM] * 3,
        out_specs=(SMEM,) * 3,
        name="children",
    )(leaf, owners, rel)


GROUP = 8
DEPTH = 2 * SLICE


def product_kernel(r_ref, count_ref, slot_ref, block_ref, a_ref, b_ref, *refs):
    outs = refs[:4]
    raw_ref, z_ref, acc_ref, sems = refs[4:]
    y, core = r_ref[0] // 2, lax.rem(r_ref[0], 2)
    count = count_ref[0]

    def fetch(i):
        slot = slot_ref[i]
        return (
            pltpu.make_async_copy(a_ref.at[slot], raw_ref.at[i, pl.ds(0, SLICE)], sems.at[i]),
            pltpu.make_async_copy(b_ref.at[slot], raw_ref.at[i, pl.ds(SLICE, SLICE)], sems.at[SLOTS + i]),
        )

    @pl.loop(0, count)
    def _(i):
        for c in fetch(i):
            c.start()

    acc_ref[...] = jnp.zeros_like(acc_ref)
    groups = (count + GROUP - 1) // GROUP

    @pl.loop(0, groups)
    def _(g):
        z_ref[...] = jnp.zeros_like(z_ref)
        for i in range(GROUP):
            n = g * GROUP + i

            @pl.when(n < count)
            def _():
                for c in fetch(n):
                    c.wait()
                for p in range(P_SIZE):
                    f = block_ref[n * P_SIZE + p]
                    at = lax.rem(f, 2) * 4 + f // 2
                    z_ref[i * DEPTH : (i + 1) * DEPTH, pl.ds(pl.multiple_of(at * BS, BS), BS)] = raw_ref[
                        n, :, p * BS : (p + 1) * BS
                    ]

        z = z_ref[...]
        half = z_ref[:, pl.ds(pl.multiple_of(core * 4 * BS, 4 * BS), 4 * BS)]
        acc_ref[...] += lax.dot_general(z, half, (((0,), (0,)), ((), ())), preferred_element_type=F32)

    for s in range(4):
        at = pl.ds(pl.multiple_of(lax.rem(y + s, 4) * BS, BS), BS)
        for place in range(FB):
            f = 2 * (place % 4) + place // 4
            outs[s][f * BS : (f + 1) * BS, :] = acc_ref[place * BS : (place + 1) * BS, at]


def product(r, count, slots, blocks, a, b):
    piece = jax.ShapeDtypeStruct((FB * BS, BS), F32)
    return pl.pallas_call(
        product_kernel,
        out_shape=(piece,) * 4,
        in_specs=[SMEM] * 4 + [ANY, ANY],
        out_specs=(VMEM,) * 4,
        scratch_shapes=[
            pltpu.VMEM((SLOTS, DEPTH, PANEL), BF16),
            pltpu.VMEM((GROUP * DEPTH, FB * BS), BF16),
            pltpu.VMEM((FB * BS, 4 * BS), F32),
            pltpu.SemaphoreType.DMA((2 * SLOTS,)),
        ],
        compiler_params=PARAMS,
        name="product",
    )(r, count, slots, blocks, a, b)


def shift_row(x, s):
    return lax.ppermute(x, "row", [(i, (i + s) % ROWS) for i in range(ROWS)])


def shift_y(x, s):
    return lax.ppermute(x, "row", [(i, (i + 2 * s) % ROWS) for i in range(ROWS)])


def swap_core(x):
    return lax.ppermute(x, "row", [(i, i ^ 1) for i in range(ROWS)])


def on_device(diag_blocks, panel, parent, rel, front):
    r = lax.axis_index("row").reshape(1)
    leaf = lax.axis_index("leaf").reshape(1)
    owners = parent.reshape(LEAVES * K)
    my_owners = lax.dynamic_slice(owners, (leaf[0] * K,), (K,))
    pieces = split(r, panel[0])
    pieces = [pieces[0]] + [shift_row(pieces[s], s) for s in range(1, ROWS)]
    factors, inverse = factor(diag_blocks[0])
    solved = solve(r, inverse, pieces)
    by_row, by_column = solved[:ROWS], solved[ROWS:]
    by_column = [by_column[0]] + [shift_row(by_column[s], s) for s in range(1, ROWS)]
    sent = outgoing(r, my_owners, by_column)
    by_row, sent, owners, rel = lax.optimization_barrier((by_row, sent, owners, rel))
    received = lax.all_to_all(
        sent.reshape(LEAVES, MOST, SLICE, PANEL), "leaf", split_axis=0, concat_axis=0, tiled=True
    ).reshape(SLOTS, SLICE, PANEL)
    by_row = [by_row[0]] + [shift_row(by_row[s], s) for s in range(1, ROWS)]
    factor_panel = join(r, by_row)
    count, slots, blocks = children(leaf, owners, rel.reshape(LEAVES * K * P_SIZE))
    other = swap_core(received)
    sums = product(r, count, slots, blocks, received, other)
    new_front = front[0] - sums[0]
    for s in range(1, 4):
        new_front = new_front - shift_y(sums[s], s)
    return (factors[None], factor_panel[None], new_front[None])


def solution(mesh):
    in_specs = (
        P("leaf", "row", None, None),
        P("leaf", None, "row", None),
        P(),
        P(),
        P("leaf", None, "row"),
    )
    out_specs = (P("leaf", "row", None, None), P("leaf", None, "row", None), P("leaf", None, "row"))
    return jax.shard_map(
        on_device, mesh=mesh, in_specs=in_specs, out_specs=out_specs, check_vma=False
    )
```

```python
import functools

import jax
import jax.numpy as jnp
from jax import lax
from jax.experimental import pallas as pl
from jax.experimental.pallas import tpu as pltpu
from jax.sharding import PartitionSpec as P

W = 256
BS = 128
FB = 8
P_SIZE = 6
K = 24
LEAVES = 32
ROWS = 8
OWN = K // ROWS
PANEL = P_SIZE * BS
PART = PANEL // ROWS
HALF = W // 2
SLICE = HALF // ROWS
MOST = 2
SLOTS = LEAVES * MOST
NB = 64
HI = lax.Precision.HIGHEST
F32 = jnp.float32
BF16 = jnp.bfloat16

ANY = pl.BlockSpec(memory_space=pl.ANY)
VMEM = pl.BlockSpec(memory_space=pltpu.VMEM)
SMEM = pl.BlockSpec(memory_space=pltpu.SMEM)
PARAMS = pltpu.CompilerParams(vmem_limit_bytes=56 * 2**20)


def mm(a, b):
    return lax.dot_general(a, b, (((1,), (0,)), ((), ())), precision=HI, preferred_element_type=F32)


def two_parts(x):
    high = x.astype(BF16)
    return high, (x - high.astype(F32)).astype(BF16)


def mm_turned(a, b):
    dot = lambda x, y: lax.dot_general(x, y, (((1,), (1,)), ((), ())), preferred_element_type=F32)
    (ah, al), (bh, bl) = two_parts(a), two_parts(b)
    return dot(ah, bh) + (dot(ah, bl) + dot(al, bh))


def lanes(x, at):
    return jnp.broadcast_to(x[:, at : at + 1], (8, 128))


def sublanes(x, at):
    return jnp.broadcast_to(x[at : at + 1, :], (8, 128))


def eliminate(tiles, offset, nb):
    sub = lax.broadcasted_iota(jnp.int32, (8, 128), 0)
    for g in range(nb // 8):
        at = offset + 8 * g
        rows = [[sublanes(ts[g], i) for i in range(8)] for ts in tiles]
        pivots = []
        for ts in tiles:
            cols = [lanes(ts[g], at + j) for j in range(8)]
            pivots.append([[sublanes(cols[j], i) for j in range(i + 1)] for i in range(8)])
        for ts, t, p in zip(tiles, rows, pivots):
            f, inv = [[None] * 8 for _ in range(8)], []
            for j in range(8):
                inv.append(1.0 / p[j][j])
                for i in range(j + 1, 8):
                    f[i][j] = p[i][j] * inv[j]
                for i in range(j + 1, 8):
                    for k in range(j + 1, i + 1):
                        p[i][k] = p[i][k] - f[i][j] * p[k][j]
                    t[i] = t[i] - f[i][j] * t[j]
            w = [t[i] * inv[i] for i in range(8)]
            for i in range(7, -1, -1):
                for j in range(i):
                    w[j] = w[j] - f[i][j] * w[i]
            done = t[0]
            for i in range(1, 8):
                done = jnp.where(sub == i, t[i], done)
            ts[g] = done
            for below in range(g + 1, nb // 8):
                new = ts[below]
                for i in range(8):
                    new = new - lanes(ts[below], at + i) * w[i]
                ts[below] = new
    return tiles


def factor_steps(first, last, s_ref, l_ref, v_ref, base):
    n, w = s_ref.shape[0], s_ref.shape[2]
    lane = lax.broadcasted_iota(jnp.int32, (NB, 128), 1)
    sub = lax.broadcasted_iota(jnp.int32, (NB, 128), 0)
    for k in range(first, last):
        lo, hi = k * NB, (k + 1) * NB
        here = slice(lo - base, hi - base)
        off = lo % 128
        other = NB - off
        tile = slice(lo - off, lo - off + 128)
        own = (lane >= off) & (lane < off + NB)
        eye = (lane - other == sub).astype(F32)
        tiles = []
        for m in range(n):
            b = jnp.where(own, s_ref[m, here, tile], eye)
            tiles.append([b[8 * t : 8 * t + 8] for t in range(NB // 8)])
        tiles = eliminate(tiles, off, NB)
        for m in range(n):
            b = jnp.concatenate(tiles[m], axis=0)
            d = jnp.sum(jnp.where(lane - off == sub, b, 0.0), axis=1, keepdims=True)
            b = b * (1.0 / jnp.sqrt(d))
            up, inv = b[:, off : off + NB], b[:, other : other + NB]
            up = jnp.where(lane[:, :NB] >= sub[:, :NB], up, 0.0)
            inv = jnp.where(lane[:, :NB] <= sub[:, :NB], inv, 0.0)
            g = mm(inv, s_ref[m, here, :])
            left = [g[:, :lo]] if k else []
            right = [g[:, hi:]] if hi < w else []
            r = jnp.concatenate(left + [inv] + right, axis=1)
            col = lax.broadcasted_iota(jnp.int32, (NB, w), 1)
            v_ref[m, lo - first * NB : hi - first * NB, :] = jnp.where(col < hi, r, 0.0)[:, : v_ref.shape[2]]
            zero = [jnp.zeros((NB, lo), F32)] if k else []
            ut = jnp.concatenate(zero + [up] + right, axis=1).T
            l_ref[m, :, lo:hi] = ut
            if hi < w:
                rest = s_ref[m, hi - base :, :]
                at = lax.broadcasted_iota(jnp.int32, rest.shape, 1)
                rest = jnp.where((at >= lo) & (at < hi), 0.0, rest)
                s_ref[m, hi - base :, :] = rest - mm(ut[hi:, :], r)


def factor_head_kernel(a_ref, l_ref, v_ref, rest_ref, s_ref):
    s_ref[...] = a_ref[...]
    factor_steps(0, HALF // NB, s_ref, l_ref, v_ref, 0)
    rest_ref[...] = s_ref[:, HALF:, :]


def factor_tail_kernel(head_ref, rest_ref, l_ref, v_ref, s_ref):
    s_ref[...] = rest_ref[...]
    l_ref[:, :, :HALF] = head_ref[...]
    factor_steps(HALF // NB, W // NB, s_ref, l_ref, v_ref, HALF)


def factor_head(a):
    shapes = ((OWN, W, HALF), (OWN, HALF, HALF), (OWN, W - HALF, W))
    return pl.pallas_call(
        factor_head_kernel,
        out_shape=tuple(jax.ShapeDtypeStruct(x, F32) for x in shapes),
        in_specs=[VMEM],
        out_specs=(VMEM,) * 3,
        scratch_shapes=[pltpu.VMEM(a.shape, F32)],
        compiler_params=PARAMS,
        name="factor_head",
    )(a)


def factor_tail(head, rest):
    shapes = ((OWN, W, W), (OWN, W - HALF, W))
    return pl.pallas_call(
        factor_tail_kernel,
        out_shape=tuple(jax.ShapeDtypeStruct(x, F32) for x in shapes),
        in_specs=[VMEM] * 2,
        out_specs=(VMEM,) * 2,
        scratch_shapes=[pltpu.VMEM(rest.shape, F32)],
        compiler_params=PARAMS,
        name="factor_tail",
    )(head, rest)


def split_kernel(half, r_ref, panel_ref, *refs):
    outs, sems = refs[:-1], refs[-1]
    copies = []
    for s in range(ROWS):
        to = lax.rem(r_ref[0] + s, ROWS)
        source = panel_ref.at[pl.ds(to * OWN, OWN), :, half * HALF : (half + 1) * HALF]
        copies.append(pltpu.make_async_copy(source, outs[s], sems.at[s]))
    for c in copies:
        c.start()
    for c in copies:
        c.wait()


def split(r, panel, half):
    piece = jax.ShapeDtypeStruct((OWN, PART, HALF), panel.dtype)
    return pl.pallas_call(
        functools.partial(split_kernel, half),
        out_shape=(piece,) * ROWS,
        in_specs=[SMEM, ANY],
        out_specs=(VMEM,) * ROWS,
        scratch_shapes=[pltpu.SemaphoreType.DMA((ROWS,))],
        compiler_params=PARAMS,
        name="split",
    )(r, panel)


def join_kernel(r_ref, *refs):
    pieces, out_ref, sems = refs[:ROWS], refs[ROWS], refs[ROWS + 1]
    copies = []
    for s in range(ROWS):
        source = lax.rem(r_ref[0] + ROWS - s, ROWS)
        copies.append(
            pltpu.make_async_copy(pieces[s], out_ref.at[pl.ds(source * OWN, OWN)], sems.at[s])
        )
    for c in copies:
        c.start()
    for c in copies:
        c.wait()


def join(r, pieces):
    return pl.pallas_call(
        join_kernel,
        out_shape=jax.ShapeDtypeStruct((K,) + pieces[0].shape[1:], pieces[0].dtype),
        in_specs=[SMEM] + [ANY] * ROWS,
        out_specs=VMEM,
        scratch_shapes=[pltpu.SemaphoreType.DMA((ROWS,))],
        compiler_params=PARAMS,
        name="join",
    )(r, *pieces)


def place_rows(r, halves, p_ref, sems):
    copies = []
    for h, pieces in enumerate(halves):
        for s in range(ROWS):
            source = lax.rem(r + ROWS - s, ROWS)
            at = pl.ds(pl.multiple_of(source * PART, PART), PART)
            to = p_ref.at[:, at, h * HALF : (h + 1) * HALF]
            copies.append(pltpu.make_async_copy(pieces[s], to, sems.at[h, s]))
    return copies


def solve_kernel(halves, r_ref, v_ref, *refs):
    n = halves * ROWS
    pieces, outs = [refs[h * ROWS : (h + 1) * ROWS] for h in range(halves)], refs[n : n + ROWS]
    t_ref, p_ref, sems = refs[n + ROWS :]
    r = r_ref[0]
    copies = place_rows(r, pieces, p_ref, sems)
    for c in copies:
        c.start()
    for c in copies:
        c.wait()
    for m in range(OWN):
        t_ref[m] = mm_turned(v_ref[m], p_ref[m]).astype(BF16)
    for s in range(ROWS):
        to = lax.rem(r + s, ROWS)
        outs[s][...] = t_ref[:, pl.ds(pl.multiple_of(to * SLICE, SLICE), SLICE), :]


def solve(r, inverse, halves):
    n = len(halves)
    piece = jax.ShapeDtypeStruct((OWN, SLICE, PANEL), BF16)
    *outs, turned = pl.pallas_call(
        functools.partial(solve_kernel, n),
        out_shape=(piece,) * ROWS + (jax.ShapeDtypeStruct((OWN, HALF, PANEL), BF16),),
        in_specs=[SMEM, VMEM] + [ANY] * (n * ROWS),
        out_specs=(VMEM,) * (ROWS + 1),
        scratch_shapes=[pltpu.VMEM((OWN, PANEL, n * HALF), F32), pltpu.SemaphoreType.DMA((n, ROWS))],
        compiler_params=PARAMS,
        name="solve",
    )(r, inverse, *[p for half in halves for p in half])
    return outs, turned


def turn_kernel(r_ref, a_ref, b_ref, *refs):
    outs, x_ref = refs[:ROWS], refs[ROWS]
    for m in range(OWN):
        x_ref[m, :, :HALF] = a_ref[m].T
        x_ref[m, :, HALF:] = b_ref[m].T
    for s in range(ROWS):
        to = lax.rem(r_ref[0] + s, ROWS)
        outs[s][...] = x_ref[:, pl.ds(pl.multiple_of(to * PART, PART), PART), :]


def turn(r, a, b):
    return pl.pallas_call(
        turn_kernel,
        out_shape=(jax.ShapeDtypeStruct((OWN, PART, W), BF16),) * ROWS,
        in_specs=[SMEM, VMEM, VMEM],
        out_specs=(VMEM,) * ROWS,
        scratch_shapes=[pltpu.VMEM((OWN, PANEL, W), BF16)],
        compiler_params=PARAMS,
        name="turn",
    )(r, a, b)


def outgoing_kernel(r_ref, owner_ref, *refs):
    pieces, out_ref = refs[:ROWS], refs[ROWS]
    used, place, sems = refs[ROWS + 1 :]
    for a in range(LEAVES):
        used[a] = 0
    for k in range(K):
        a = owner_ref[k]
        place[k] = MOST * a + used[a]
        used[a] = used[a] + 1
    copies = []
    for s in range(ROWS):
        source = lax.rem(r_ref[0] + ROWS - s, ROWS)
        for i in range(OWN):
            copies.append(
                pltpu.make_async_copy(
                    pieces[s].at[i], out_ref.at[place[source * OWN + i]], sems.at[s, i]
                )
            )
            copies[-1].start()
    for c in copies:
        c.wait()


def outgoing(r, owners, pieces):
    return pl.pallas_call(
        outgoing_kernel,
        out_shape=jax.ShapeDtypeStruct((SLOTS, SLICE, PANEL), BF16),
        in_specs=[SMEM, SMEM] + [ANY] * ROWS,
        out_specs=VMEM,
        scratch_shapes=[
            pltpu.SMEM((LEAVES,), jnp.int32),
            pltpu.SMEM((K,), jnp.int32),
            pltpu.SemaphoreType.DMA((ROWS, OWN)),
        ],
        compiler_params=PARAMS,
        name="outgoing",
    )(r, owners, *pieces)


def children_kernel(leaf_ref, owner_ref, rel_ref, out_ref):
    me = leaf_ref[0]
    node = lax.broadcasted_iota(jnp.int32, (LEAVES, K), 1)
    hit = owner_ref[...] == me
    first = jnp.min(jnp.where(hit, node, K), axis=1, keepdims=True)
    second = jnp.max(jnp.where(hit, node, -1), axis=1, keepdims=True)
    filled = ((first < K).astype(jnp.int32), (second > first).astype(jnp.int32))
    entry = lax.broadcasted_iota(jnp.int32, (LEAVES, K * P_SIZE), 1)
    lane = lax.broadcasted_iota(jnp.int32, (LEAVES, 128), 1)
    f = rel_ref[...]
    place = lax.rem(f, 2) * 4 + f // 2
    out = jnp.zeros((LEAVES, 128), jnp.int32)
    for s, at in enumerate((first, second)):
        out = jnp.where(lane == s, filled[s], out)
        for p in range(P_SIZE):
            block = jnp.sum(jnp.where(entry == at * P_SIZE + p, place, 0), axis=1, keepdims=True)
            out = jnp.where(lane == MOST + s * P_SIZE + p, block, out)
    out_ref[...] = out


def children(leaf, owners, rel):
    return pl.pallas_call(
        children_kernel,
        out_shape=jax.ShapeDtypeStruct((LEAVES, 128), jnp.int32),
        in_specs=[SMEM, VMEM, VMEM],
        out_specs=VMEM,
        name="children",
    )(leaf, owners, rel)


GROUP = 8
DEPTH = 2 * SLICE


def product_kernel(last, r_ref, table_ref, a_ref, b_ref, *refs):
    raw_ref, z_ref, slot_ref, sems = refs[-4:]
    if last:
        before_ref, outs, acc_ref = refs[0], refs[1:5], refs[5]
    else:
        acc_ref = refs[0]
    y, core = r_ref[0] // 2, lax.rem(r_ref[0], 2)

    def fetch(slot, i):
        return (
            pltpu.make_async_copy(a_ref.at[slot], raw_ref.at[i, pl.ds(0, SLICE)], sems.at[i]),
            pltpu.make_async_copy(b_ref.at[slot], raw_ref.at[i, pl.ds(SLICE, SLICE)], sems.at[SLOTS + i]),
        )

    def from_leaf(j, count):
        for s in range(MOST):
            filled = table_ref[j, s]

            @pl.when(filled == 1)
            def _():
                slot_ref[count] = MOST * j + s
                for c in fetch(MOST * j + s, count):
                    c.start()

            count = count + filled
        return count

    count = lax.fori_loop(0, LEAVES, from_leaf, 0)
    acc_ref[...] = before_ref[...] if last else jnp.zeros_like(acc_ref)
    groups = (count + GROUP - 1) // GROUP

    @pl.loop(0, groups)
    def _(g):
        z_ref[...] = jnp.zeros_like(z_ref)
        for i in range(GROUP):
            n = g * GROUP + i

            @pl.when(n < count)
            def _():
                slot = slot_ref[n]
                for c in fetch(slot, n):
                    c.wait()
                for p in range(P_SIZE):
                    at = table_ref[slot // MOST, MOST + lax.rem(slot, MOST) * P_SIZE + p]
                    z_ref[i * DEPTH : (i + 1) * DEPTH, pl.ds(pl.multiple_of(at * BS, BS), BS)] = raw_ref[
                        n, :, p * BS : (p + 1) * BS
                    ]

        z = z_ref[...]
        half = z_ref[:, pl.ds(pl.multiple_of(core * 4 * BS, 4 * BS), 4 * BS)]
        acc_ref[...] += lax.dot_general(z, half, (((0,), (0,)), ((), ())), preferred_element_type=F32)

    if last:
        for s in range(4):
            at = pl.ds(pl.multiple_of(lax.rem(y + s, 4) * BS, BS), BS)
            for place in range(FB):
                f = 2 * (place % 4) + place // 4
                outs[s][f * BS : (f + 1) * BS, :] = acc_ref[place * BS : (place + 1) * BS, at]


def product(r, table, a, b, before=None):
    last = before is not None
    total = (FB * BS, 4 * BS)
    piece = jax.ShapeDtypeStruct((FB * BS, BS), F32)
    return pl.pallas_call(
        functools.partial(product_kernel, last),
        out_shape=(piece,) * 4 if last else jax.ShapeDtypeStruct(total, F32),
        in_specs=[SMEM] * 2 + [ANY, ANY] + ([VMEM] if last else []),
        out_specs=(VMEM,) * 4 if last else VMEM,
        scratch_shapes=([pltpu.VMEM(total, F32)] if last else [])
        + [
            pltpu.VMEM((SLOTS, DEPTH, PANEL), BF16),
            pltpu.VMEM((GROUP * DEPTH, FB * BS), BF16),
            pltpu.SMEM((SLOTS,), jnp.int32),
            pltpu.SemaphoreType.DMA((2 * SLOTS,)),
        ],
        compiler_params=PARAMS,
        name="product",
    )(r, table, a, b, *([before] if last else []))


def shift_row(x, s):
    return lax.ppermute(x, "row", [(i, (i + s) % ROWS) for i in range(ROWS)])


def shift_y(x, s):
    return lax.ppermute(x, "row", [(i, (i + 2 * s) % ROWS) for i in range(ROWS)])


def swap_core(x):
    return lax.ppermute(x, "row", [(i, i ^ 1) for i in range(ROWS)])


def over_row(pieces):
    return [pieces[0]] + [shift_row(pieces[s], s) for s in range(1, ROWS)]


def to_parents(sent):
    sent = sent.reshape(LEAVES, MOST, SLICE, PANEL)
    received = lax.all_to_all(sent, "leaf", split_axis=0, concat_axis=0, tiled=True)
    return received.reshape(SLOTS, SLICE, PANEL)


def on_device(diag_blocks, panel, parent, rel, front):
    r = lax.axis_index("row").reshape(1)
    leaf = lax.axis_index("leaf").reshape(1)
    owners = parent.reshape(LEAVES * K)
    my_owners = lax.dynamic_slice(owners, (leaf[0] * K,), (K,))
    pieces = [over_row(split(r, panel[0], half)) for half in range(2)]
    head, inverse, rest = factor_head(diag_blocks[0])
    outs, turned = solve(r, inverse, pieces[:1])
    sent = outgoing(r, my_owners, over_row(outs))
    sent, head, rest = lax.optimization_barrier((sent, head, rest))
    received = to_parents(sent)
    factors, inverse = factor_tail(head, rest)
    outs, turned_too = solve(r, inverse, pieces)
    sent = outgoing(r, my_owners, over_row(outs))
    received, sent, turned, turned_too, parent, rel = lax.optimization_barrier(
        (received, sent, turned, turned_too, parent, rel)
    )
    received_too = to_parents(sent)
    table = children(leaf, parent.reshape(LEAVES, K), rel.reshape(LEAVES, K * P_SIZE))
    total = product(r, table, received, swap_core(received))
    factor_panel = join(r, over_row(turn(r, turned, turned_too)))
    received_too, total, factor_panel = lax.optimization_barrier((received_too, total, factor_panel))
    sums = product(r, table, received_too, swap_core(received_too), total)
    new_front = front[0] - sums[0]
    for s in range(1, 4):
        new_front = new_front - shift_y(sums[s], s)
    return (factors[None], factor_panel[None], new_front[None])


def solution(mesh):
    in_specs = (
        P("leaf", "row", None, None),
        P("leaf", None, "row", None),
        P(),
        P(),
        P("leaf", None, "row"),
    )
    out_specs = (P("leaf", "row", None, None), P("leaf", None, "row", None), P("leaf", None, "row"))
    return jax.shard_map(
        on_device, mesh=mesh, in_specs=in_specs, out_specs=out_specs, check_vma=False
    )
```

```python
import functools

import jax
import jax.numpy as jnp
from jax import lax
from jax.experimental import pallas as pl
from jax.experimental.pallas import tpu as pltpu
from jax.sharding import PartitionSpec as P

W = 256
BS = 128
FB = 8
P_SIZE = 6
K = 24
LEAVES = 32
ROWS = 8
OWN = K // ROWS
PANEL = P_SIZE * BS
PART = PANEL // ROWS
HALF = W // 2
SLICE = HALF // ROWS
MOST = 2
SLOTS = LEAVES * MOST
NB = 64
HI = lax.Precision.HIGHEST
F32 = jnp.float32
BF16 = jnp.bfloat16

ANY = pl.BlockSpec(memory_space=pl.ANY)
VMEM = pl.BlockSpec(memory_space=pltpu.VMEM)
SMEM = pl.BlockSpec(memory_space=pltpu.SMEM)
PARAMS = pltpu.CompilerParams(vmem_limit_bytes=56 * 2**20)


def mm(a, b):
    return lax.dot_general(a, b, (((1,), (0,)), ((), ())), precision=HI, preferred_element_type=F32)


def two_parts(x):
    high = x.astype(BF16)
    return high, (x - high.astype(F32)).astype(BF16)


def mm_turned(a, b):
    dot = lambda x, y: lax.dot_general(x, y, (((1,), (1,)), ((), ())), preferred_element_type=F32)
    (ah, al), (bh, bl) = two_parts(a), two_parts(b)
    return dot(ah, bh) + (dot(ah, bl) + dot(al, bh))


def lanes(x, at):
    return jnp.broadcast_to(x[:, at : at + 1], (8, 128))


def sublanes(x, at):
    return jnp.broadcast_to(x[at : at + 1, :], (8, 128))


def eliminate(tiles, offset, nb):
    sub = lax.broadcasted_iota(jnp.int32, (8, 128), 0)
    for g in range(nb // 8):
        at = offset + 8 * g
        rows = [[sublanes(ts[g], i) for i in range(8)] for ts in tiles]
        pivots = []
        for ts in tiles:
            cols = [lanes(ts[g], at + j) for j in range(8)]
            pivots.append([[sublanes(cols[j], i) for j in range(i + 1)] for i in range(8)])
        for ts, t, p in zip(tiles, rows, pivots):
            f, inv = [[None] * 8 for _ in range(8)], []
            for j in range(8):
                inv.append(1.0 / p[j][j])
                for i in range(j + 1, 8):
                    f[i][j] = p[i][j] * inv[j]
                for i in range(j + 1, 8):
                    for k in range(j + 1, i + 1):
                        p[i][k] = p[i][k] - f[i][j] * p[k][j]
                    t[i] = t[i] - f[i][j] * t[j]
            w = [t[i] * inv[i] for i in range(8)]
            for i in range(7, -1, -1):
                for j in range(i):
                    w[j] = w[j] - f[i][j] * w[i]
            done = t[0]
            for i in range(1, 8):
                done = jnp.where(sub == i, t[i], done)
            ts[g] = done
            for below in range(g + 1, nb // 8):
                new = ts[below]
                for i in range(8):
                    new = new - lanes(ts[below], at + i) * w[i]
                ts[below] = new
    return tiles


def factor_steps(first, last, s_ref, l_ref, v_ref, base):
    n, w = s_ref.shape[0], s_ref.shape[2]
    lane = lax.broadcasted_iota(jnp.int32, (NB, 128), 1)
    sub = lax.broadcasted_iota(jnp.int32, (NB, 128), 0)
    for k in range(first, last):
        lo, hi = k * NB, (k + 1) * NB
        here = slice(lo - base, hi - base)
        off = lo % 128
        other = NB - off
        tile = slice(lo - off, lo - off + 128)
        own = (lane >= off) & (lane < off + NB)
        eye = (lane - other == sub).astype(F32)
        tiles = []
        for m in range(n):
            b = jnp.where(own, s_ref[m, here, tile], eye)
            tiles.append([b[8 * t : 8 * t + 8] for t in range(NB // 8)])
        tiles = eliminate(tiles, off, NB)
        for m in range(n):
            b = jnp.concatenate(tiles[m], axis=0)
            d = jnp.sum(jnp.where(lane - off == sub, b, 0.0), axis=1, keepdims=True)
            b = b * (1.0 / jnp.sqrt(d))
            up, inv = b[:, off : off + NB], b[:, other : other + NB]
            up = jnp.where(lane[:, :NB] >= sub[:, :NB], up, 0.0)
            inv = jnp.where(lane[:, :NB] <= sub[:, :NB], inv, 0.0)
            g = mm(inv, s_ref[m, here, :])
            left = [g[:, :lo]] if k else []
            right = [g[:, hi:]] if hi < w else []
            r = jnp.concatenate(left + [inv] + right, axis=1)
            col = lax.broadcasted_iota(jnp.int32, (NB, w), 1)
            v_ref[m, lo - first * NB : hi - first * NB, :] = jnp.where(col < hi, r, 0.0)[:, : v_ref.shape[2]]
            zero = [jnp.zeros((NB, lo), F32)] if k else []
            ut = jnp.concatenate(zero + [up] + right, axis=1).T
            l_ref[m, :, lo:hi] = ut
            if hi < w:
                rest = s_ref[m, hi - base :, :]
                at = lax.broadcasted_iota(jnp.int32, rest.shape, 1)
                rest = jnp.where((at >= lo) & (at < hi), 0.0, rest)
                s_ref[m, hi - base :, :] = rest - mm(ut[hi:, :], r)


def factor_head_kernel(a_ref, l_ref, v_ref, rest_ref, s_ref):
    s_ref[...] = a_ref[...]
    factor_steps(0, HALF // NB, s_ref, l_ref, v_ref, 0)
    rest_ref[...] = s_ref[:, HALF:, :]


def factor_tail_kernel(head_ref, rest_ref, l_ref, v_ref, s_ref):
    s_ref[...] = rest_ref[...]
    l_ref[:, :, :HALF] = head_ref[...]
    factor_steps(HALF // NB, W // NB, s_ref, l_ref, v_ref, HALF)


def factor_head(a):
    shapes = ((OWN, W, HALF), (OWN, HALF, HALF), (OWN, W - HALF, W))
    return pl.pallas_call(
        factor_head_kernel,
        out_shape=tuple(jax.ShapeDtypeStruct(x, F32) for x in shapes),
        in_specs=[VMEM],
        out_specs=(VMEM,) * 3,
        scratch_shapes=[pltpu.VMEM(a.shape, F32)],
        compiler_params=PARAMS,
        name="factor_head",
    )(a)


def factor_tail(head, rest):
    shapes = ((OWN, W, W), (OWN, W - HALF, W))
    return pl.pallas_call(
        factor_tail_kernel,
        out_shape=tuple(jax.ShapeDtypeStruct(x, F32) for x in shapes),
        in_specs=[VMEM] * 2,
        out_specs=(VMEM,) * 2,
        scratch_shapes=[pltpu.VMEM(rest.shape, F32)],
        compiler_params=PARAMS,
        name="factor_tail",
    )(head, rest)


def split_kernel(half, r_ref, panel_ref, *refs):
    outs, sems = refs[:-1], refs[-1]
    copies = []
    for s in range(ROWS):
        to = lax.rem(r_ref[0] + s, ROWS)
        source = panel_ref.at[pl.ds(to * OWN, OWN), :, half * HALF : (half + 1) * HALF]
        copies.append(pltpu.make_async_copy(source, outs[s], sems.at[s]))
    for c in copies:
        c.start()
    for c in copies:
        c.wait()


def split(r, panel, half):
    piece = jax.ShapeDtypeStruct((OWN, PART, HALF), panel.dtype)
    return pl.pallas_call(
        functools.partial(split_kernel, half),
        out_shape=(piece,) * ROWS,
        in_specs=[SMEM, ANY],
        out_specs=(VMEM,) * ROWS,
        scratch_shapes=[pltpu.SemaphoreType.DMA((ROWS,))],
        compiler_params=PARAMS,
        name="split",
    )(r, panel)


def join_kernel(r_ref, *refs):
    pieces, out_ref, sems = refs[:ROWS], refs[ROWS], refs[ROWS + 1]
    copies = []
    for s in range(ROWS):
        source = lax.rem(r_ref[0] + ROWS - s, ROWS)
        copies.append(
            pltpu.make_async_copy(pieces[s], out_ref.at[pl.ds(source * OWN, OWN)], sems.at[s])
        )
    for c in copies:
        c.start()
    for c in copies:
        c.wait()


def join(r, pieces):
    return pl.pallas_call(
        join_kernel,
        out_shape=jax.ShapeDtypeStruct((K,) + pieces[0].shape[1:], pieces[0].dtype),
        in_specs=[SMEM] + [ANY] * ROWS,
        out_specs=VMEM,
        scratch_shapes=[pltpu.SemaphoreType.DMA((ROWS,))],
        compiler_params=PARAMS,
        name="join",
    )(r, *pieces)


def place_rows(r, halves, p_ref, sems):
    copies = []
    for h, pieces in enumerate(halves):
        for s in range(ROWS):
            source = lax.rem(r + ROWS - s, ROWS)
            at = pl.ds(pl.multiple_of(source * PART, PART), PART)
            to = p_ref.at[:, at, h * HALF : (h + 1) * HALF]
            copies.append(pltpu.make_async_copy(pieces[s], to, sems.at[h, s]))
    return copies


def solve_kernel(halves, r_ref, v_ref, *refs):
    n = halves * ROWS
    pieces, outs = [refs[h * ROWS : (h + 1) * ROWS] for h in range(halves)], refs[n : n + ROWS]
    t_ref, p_ref, sems = refs[n + ROWS :]
    r = r_ref[0]
    copies = place_rows(r, pieces, p_ref, sems)
    for c in copies:
        c.start()
    for c in copies:
        c.wait()
    for m in range(OWN):
        t_ref[m] = mm_turned(v_ref[m], p_ref[m]).astype(BF16)
    for s in range(ROWS):
        to = lax.rem(r + s, ROWS)
        outs[s][...] = t_ref[:, pl.ds(pl.multiple_of(to * SLICE, SLICE), SLICE), :]


def solve(r, inverse, halves):
    n = len(halves)
    piece = jax.ShapeDtypeStruct((OWN, SLICE, PANEL), BF16)
    *outs, turned = pl.pallas_call(
        functools.partial(solve_kernel, n),
        out_shape=(piece,) * ROWS + (jax.ShapeDtypeStruct((OWN, HALF, PANEL), BF16),),
        in_specs=[SMEM, VMEM] + [ANY] * (n * ROWS),
        out_specs=(VMEM,) * (ROWS + 1),
        scratch_shapes=[pltpu.VMEM((OWN, PANEL, n * HALF), F32), pltpu.SemaphoreType.DMA((n, ROWS))],
        compiler_params=PARAMS,
        name="solve",
    )(r, inverse, *[p for half in halves for p in half])
    return outs, turned


def turn_kernel(r_ref, a_ref, b_ref, *refs):
    outs, x_ref = refs[:ROWS], refs[ROWS]
    for m in range(OWN):
        x_ref[m, :, :HALF] = a_ref[m].T
        x_ref[m, :, HALF:] = b_ref[m].T
    for s in range(ROWS):
        to = lax.rem(r_ref[0] + s, ROWS)
        outs[s][...] = x_ref[:, pl.ds(pl.multiple_of(to * PART, PART), PART), :]


def turn(r, a, b):
    return pl.pallas_call(
        turn_kernel,
        out_shape=(jax.ShapeDtypeStruct((OWN, PART, W), BF16),) * ROWS,
        in_specs=[SMEM, VMEM, VMEM],
        out_specs=(VMEM,) * ROWS,
        scratch_shapes=[pltpu.VMEM((OWN, PANEL, W), BF16)],
        compiler_params=PARAMS,
        name="turn",
    )(r, a, b)


def outgoing_kernel(r_ref, owner_ref, *refs):
    pieces, out_ref = refs[:ROWS], refs[ROWS]
    used, place, sems = refs[ROWS + 1 :]
    for a in range(LEAVES):
        used[a] = 0
    for k in range(K):
        a = owner_ref[k]
        place[k] = MOST * a + used[a]
        used[a] = used[a] + 1
    copies = []
    for s in range(ROWS):
        source = lax.rem(r_ref[0] + ROWS - s, ROWS)
        for i in range(OWN):
            copies.append(
                pltpu.make_async_copy(
                    pieces[s].at[i], out_ref.at[place[source * OWN + i]], sems.at[s, i]
                )
            )
            copies[-1].start()
    for c in copies:
        c.wait()


def outgoing(r, owners, pieces):
    return pl.pallas_call(
        outgoing_kernel,
        out_shape=jax.ShapeDtypeStruct((SLOTS, SLICE, PANEL), BF16),
        in_specs=[SMEM, SMEM] + [ANY] * ROWS,
        out_specs=VMEM,
        scratch_shapes=[
            pltpu.SMEM((LEAVES,), jnp.int32),
            pltpu.SMEM((K,), jnp.int32),
            pltpu.SemaphoreType.DMA((ROWS, OWN)),
        ],
        compiler_params=PARAMS,
        name="outgoing",
    )(r, owners, *pieces)


def children_kernel(leaf_ref, owner_ref, rel_ref, out_ref):
    me = leaf_ref[0]
    node = lax.broadcasted_iota(jnp.int32, (LEAVES, K), 1)
    hit = owner_ref[...] == me
    first = jnp.min(jnp.where(hit, node, K), axis=1, keepdims=True)
    second = jnp.max(jnp.where(hit, node, -1), axis=1, keepdims=True)
    filled = ((first < K).astype(jnp.int32), (second > first).astype(jnp.int32))
    entry = lax.broadcasted_iota(jnp.int32, (LEAVES, K * P_SIZE), 1)
    lane = lax.broadcasted_iota(jnp.int32, (LEAVES, 128), 1)
    f = rel_ref[...]
    place = lax.rem(f, 2) * 4 + f // 2
    out = jnp.zeros((LEAVES, 128), jnp.int32)
    for s, at in enumerate((first, second)):
        out = jnp.where(lane == s, filled[s], out)
        for p in range(P_SIZE):
            block = jnp.sum(jnp.where(entry == at * P_SIZE + p, place, 0), axis=1, keepdims=True)
            out = jnp.where(lane == MOST + s * P_SIZE + p, block, out)
    out_ref[...] = out


def children(leaf, owners, rel):
    return pl.pallas_call(
        children_kernel,
        out_shape=jax.ShapeDtypeStruct((LEAVES, 128), jnp.int32),
        in_specs=[SMEM, VMEM, VMEM],
        out_specs=VMEM,
        name="children",
    )(leaf, owners, rel)


GROUP = 8
DEPTH = 2 * SLICE


def product_kernel(last, r_ref, table_ref, a_ref, b_ref, *refs):
    raw_ref, z_ref, slot_ref, sems = refs[-4:]
    if last:
        before_ref, outs, acc_ref = refs[0], refs[1:5], refs[5]
    else:
        acc_ref = refs[0]
    y, core = r_ref[0] // 2, lax.rem(r_ref[0], 2)

    def fetch(slot, i):
        return (
            pltpu.make_async_copy(a_ref.at[slot], raw_ref.at[i, pl.ds(0, SLICE)], sems.at[i]),
            pltpu.make_async_copy(b_ref.at[slot], raw_ref.at[i, pl.ds(SLICE, SLICE)], sems.at[SLOTS + i]),
        )

    def from_leaf(j, count):
        for s in range(MOST):
            filled = table_ref[j, s]

            @pl.when(filled == 1)
            def _():
                slot_ref[count] = MOST * j + s
                for c in fetch(MOST * j + s, count):
                    c.start()

            count = count + filled
        return count

    count = lax.fori_loop(0, LEAVES, from_leaf, 0)
    acc_ref[...] = before_ref[...] if last else jnp.zeros_like(acc_ref)
    groups = (count + GROUP - 1) // GROUP

    @pl.loop(0, groups)
    def _(g):
        z_ref[...] = jnp.zeros_like(z_ref)
        for i in range(GROUP):
            n = g * GROUP + i

            @pl.when(n < count)
            def _():
                slot = slot_ref[n]
                for c in fetch(slot, n):
                    c.wait()
                for p in range(P_SIZE):
                    at = table_ref[slot // MOST, MOST + lax.rem(slot, MOST) * P_SIZE + p]
                    z_ref[i * DEPTH : (i + 1) * DEPTH, pl.ds(pl.multiple_of(at * BS, BS), BS)] = raw_ref[
                        n, :, p * BS : (p + 1) * BS
                    ]

        half = z_ref[:, pl.ds(pl.multiple_of(core * 4 * BS, 4 * BS), 4 * BS)]
        acc_ref[...] += lax.dot_general(
            half, z_ref[...], (((0,), (0,)), ((), ())), preferred_element_type=F32
        )

    if last:
        for s in range(4):
            x = acc_ref[pl.ds(pl.multiple_of(lax.rem(y + s, 4) * BS, BS), BS), :]
            if s == 0:
                outs[s][...] = x
                continue
            most = jnp.max(jnp.abs(x), axis=0, keepdims=True)
            power = jnp.ceil(jnp.log2(jnp.maximum(most, 1e-30)) - 14.998)
            outs[s][:BS, :] = to_i16(jnp.floor(x * jnp.exp2(-power) + 0.5))
            outs[s][BS:, :] = to_i16(jnp.broadcast_to(power, (16, FB * BS)))


def to_i16(x):
    return x.astype(jnp.int32).astype(jnp.int16)


def product(r, table, a, b, before=None):
    last = before is not None
    total = (4 * BS, FB * BS)
    own = jax.ShapeDtypeStruct((BS, FB * BS), F32)
    coded = jax.ShapeDtypeStruct((BS + 16, FB * BS), jnp.int16)
    return pl.pallas_call(
        functools.partial(product_kernel, last),
        out_shape=(own, coded, coded, coded) if last else jax.ShapeDtypeStruct(total, F32),
        in_specs=[SMEM] * 2 + [ANY, ANY] + ([VMEM] if last else []),
        out_specs=(VMEM,) * 4 if last else VMEM,
        scratch_shapes=([pltpu.VMEM(total, F32)] if last else [])
        + [
            pltpu.VMEM((SLOTS, DEPTH, PANEL), BF16),
            pltpu.VMEM((GROUP * DEPTH, FB * BS), BF16),
            pltpu.SMEM((SLOTS,), jnp.int32),
            pltpu.SemaphoreType.DMA((2 * SLOTS,)),
        ],
        compiler_params=PARAMS,
        name="product",
    )(r, table, a, b, *([before] if last else []))


def subtract_kernel(front_ref, own_ref, *refs):
    parts, out_ref = refs[:3], refs[3]
    for place in range(FB):
        at = slice(place * BS, (place + 1) * BS)
        total = own_ref[:, at]
        for part in parts:
            scale = jnp.exp2(part[BS:, at].astype(jnp.int32).astype(F32)[:1])
            total = total + part[:BS, at].astype(jnp.int32).astype(F32) * scale
        f = 2 * (place % 4) + place // 4
        rows = slice(f * BS, (f + 1) * BS)
        out_ref[rows, :] = front_ref[rows, :] - total.T


def subtract(front, own, parts):
    return pl.pallas_call(
        subtract_kernel,
        out_shape=jax.ShapeDtypeStruct(front.shape, F32),
        in_specs=[VMEM] * 5,
        out_specs=VMEM,
        compiler_params=PARAMS,
        name="subtract",
    )(front, own, *parts)


def shift_row(x, s):
    return lax.ppermute(x, "row", [(i, (i + s) % ROWS) for i in range(ROWS)])


def shift_y(x, s):
    return lax.ppermute(x, "row", [(i, (i + 2 * s) % ROWS) for i in range(ROWS)])


def swap_core(x):
    return lax.ppermute(x, "row", [(i, i ^ 1) for i in range(ROWS)])


def over_row(pieces):
    return [pieces[0]] + [shift_row(pieces[s], s) for s in range(1, ROWS)]


def to_parents(sent):
    sent = sent.reshape(LEAVES, MOST, SLICE, PANEL)
    received = lax.all_to_all(sent, "leaf", split_axis=0, concat_axis=0, tiled=True)
    return received.reshape(SLOTS, SLICE, PANEL)


def on_device(diag_blocks, panel, parent, rel, front):
    r = lax.axis_index("row").reshape(1)
    leaf = lax.axis_index("leaf").reshape(1)
    owners = parent.reshape(LEAVES * K)
    my_owners = lax.dynamic_slice(owners, (leaf[0] * K,), (K,))
    pieces = [over_row(split(r, panel[0], half)) for half in range(2)]
    head, inverse, rest = factor_head(diag_blocks[0])
    outs, turned = solve(r, inverse, pieces[:1])
    sent = outgoing(r, my_owners, over_row(outs))
    sent, head, rest = lax.optimization_barrier((sent, head, rest))
    received = to_parents(sent)
    factors, inverse = factor_tail(head, rest)
    outs, turned_too = solve(r, inverse, pieces)
    sent = outgoing(r, my_owners, over_row(outs))
    received, sent, turned, turned_too, parent, rel = lax.optimization_barrier(
        (received, sent, turned, turned_too, parent, rel)
    )
    received_too = to_parents(sent)
    table = children(leaf, parent.reshape(LEAVES, K), rel.reshape(LEAVES, K * P_SIZE))
    total = product(r, table, received, swap_core(received))
    factor_panel = join(r, over_row(turn(r, turned, turned_too)))
    received_too, total, factor_panel = lax.optimization_barrier((received_too, total, factor_panel))
    sums = product(r, table, received_too, swap_core(received_too), total)
    new_front = subtract(front[0], sums[0], [shift_y(sums[s], s) for s in range(1, 4)])
    return (factors[None], factor_panel[None], new_front[None])


def solution(mesh):
    in_specs = (
        P("leaf", "row", None, None),
        P("leaf", None, "row", None),
        P(),
        P(),
        P("leaf", None, "row"),
    )
    out_specs = (P("leaf", "row", None, None), P("leaf", None, "row", None), P("leaf", None, "row"))
    return jax.shard_map(
        on_device, mesh=mesh, in_specs=in_specs, out_specs=out_specs, check_vma=False
    )
```

```python
import functools

import jax
import jax.numpy as jnp
from jax import lax
from jax.experimental import pallas as pl
from jax.experimental.pallas import tpu as pltpu
from jax.sharding import PartitionSpec as P

W = 256
BS = 128
FB = 8
P_SIZE = 6
K = 24
LEAVES = 32
ROWS = 8
OWN = K // ROWS
PANEL = P_SIZE * BS
PART = PANEL // ROWS
HALF = W // 2
SLICE = HALF // ROWS
MOST = 2
SLOTS = LEAVES * MOST
NB = 64
HI = lax.Precision.HIGHEST
F32 = jnp.float32
BF16 = jnp.bfloat16

ANY = pl.BlockSpec(memory_space=pl.ANY)
VMEM = pl.BlockSpec(memory_space=pltpu.VMEM)
SMEM = pl.BlockSpec(memory_space=pltpu.SMEM)
PARAMS = pltpu.CompilerParams(vmem_limit_bytes=32 * 2**20)


def keep(arrays):
    return [pltpu.with_memory_space_constraint(x, pltpu.VMEM) for x in arrays]


def mm(a, b):
    return lax.dot_general(a, b, (((1,), (0,)), ((), ())), precision=HI, preferred_element_type=F32)


def two_parts(x):
    high = x.astype(BF16)
    return high, (x - high.astype(F32)).astype(BF16)


def mm_turned(a, b):
    dot = lambda x, y: lax.dot_general(x, y, (((1,), (1,)), ((), ())), preferred_element_type=F32)
    (ah, al), (bh, bl) = two_parts(a), two_parts(b)
    return dot(ah, bh) + (dot(ah, bl) + dot(al, bh))


def lanes(x, at):
    return jnp.broadcast_to(x[:, at : at + 1], (8, 128))


def sublanes(x, at):
    return jnp.broadcast_to(x[at : at + 1, :], (8, 128))


def eliminate(tiles, offset, nb):
    sub = lax.broadcasted_iota(jnp.int32, (8, 128), 0)
    for g in range(nb // 8):
        at = offset + 8 * g
        rows = [[sublanes(ts[g], i) for i in range(8)] for ts in tiles]
        pivots = []
        for ts in tiles:
            cols = [lanes(ts[g], at + j) for j in range(8)]
            pivots.append([[sublanes(cols[j], i) for j in range(i + 1)] for i in range(8)])
        for ts, t, p in zip(tiles, rows, pivots):
            f, inv = [[None] * 8 for _ in range(8)], []
            for j in range(8):
                inv.append(1.0 / p[j][j])
                for i in range(j + 1, 8):
                    f[i][j] = p[i][j] * inv[j]
                for i in range(j + 1, 8):
                    for k in range(j + 1, i + 1):
                        p[i][k] = p[i][k] - f[i][j] * p[k][j]
                    t[i] = t[i] - f[i][j] * t[j]
            w = [t[i] * inv[i] for i in range(8)]
            for i in range(7, -1, -1):
                for j in range(i):
                    w[j] = w[j] - f[i][j] * w[i]
            done = t[0]
            for i in range(1, 8):
                done = jnp.where(sub == i, t[i], done)
            ts[g] = done
            for below in range(g + 1, nb // 8):
                new = ts[below]
                for i in range(8):
                    new = new - lanes(ts[below], at + i) * w[i]
                ts[below] = new
    return tiles


def factor_steps(first, last, s_ref, l_ref, v_ref, base):
    n, w = s_ref.shape[0], s_ref.shape[2]
    lane = lax.broadcasted_iota(jnp.int32, (NB, 128), 1)
    sub = lax.broadcasted_iota(jnp.int32, (NB, 128), 0)
    for k in range(first, last):
        lo, hi = k * NB, (k + 1) * NB
        here = slice(lo - base, hi - base)
        off = lo % 128
        other = NB - off
        tile = slice(lo - off, lo - off + 128)
        own = (lane >= off) & (lane < off + NB)
        eye = (lane - other == sub).astype(F32)
        tiles = []
        for m in range(n):
            b = jnp.where(own, s_ref[m, here, tile], eye)
            tiles.append([b[8 * t : 8 * t + 8] for t in range(NB // 8)])
        tiles = eliminate(tiles, off, NB)
        for m in range(n):
            b = jnp.concatenate(tiles[m], axis=0)
            d = jnp.sum(jnp.where(lane - off == sub, b, 0.0), axis=1, keepdims=True)
            b = b * (1.0 / jnp.sqrt(d))
            up, inv = b[:, off : off + NB], b[:, other : other + NB]
            up = jnp.where(lane[:, :NB] >= sub[:, :NB], up, 0.0)
            inv = jnp.where(lane[:, :NB] <= sub[:, :NB], inv, 0.0)
            g = mm(inv, s_ref[m, here, :])
            left = [g[:, :lo]] if k else []
            right = [g[:, hi:]] if hi < w else []
            r = jnp.concatenate(left + [inv] + right, axis=1)
            col = lax.broadcasted_iota(jnp.int32, (NB, w), 1)
            v_ref[m, lo - first * NB : hi - first * NB, :] = jnp.where(col < hi, r, 0.0)[:, : v_ref.shape[2]]
            zero = [jnp.zeros((NB, lo), F32)] if k else []
            ut = jnp.concatenate(zero + [up] + right, axis=1).T
            l_ref[m, :, lo:hi] = ut
            if hi < w:
                rest = s_ref[m, hi - base :, :]
                at = lax.broadcasted_iota(jnp.int32, rest.shape, 1)
                rest = jnp.where((at >= lo) & (at < hi), 0.0, rest)
                s_ref[m, hi - base :, :] = rest - mm(ut[hi:, :], r)


def factor_head_kernel(a_ref, l_ref, v_ref, rest_ref, s_ref):
    s_ref[...] = a_ref[...]
    factor_steps(0, HALF // NB, s_ref, l_ref, v_ref, 0)
    rest_ref[...] = s_ref[:, HALF:, :]


def factor_tail_kernel(head_ref, rest_ref, l_ref, v_ref, s_ref):
    s_ref[...] = rest_ref[...]
    l_ref[:, :, :HALF] = head_ref[...]
    factor_steps(HALF // NB, W // NB, s_ref, l_ref, v_ref, HALF)


def factor_head(a):
    shapes = ((OWN, W, HALF), (OWN, HALF, HALF), (OWN, W - HALF, W))
    return pl.pallas_call(
        factor_head_kernel,
        out_shape=tuple(jax.ShapeDtypeStruct(x, F32) for x in shapes),
        in_specs=[VMEM],
        out_specs=(VMEM,) * 3,
        scratch_shapes=[pltpu.VMEM(a.shape, F32)],
        compiler_params=PARAMS,
        name="factor_head",
    )(a)


def factor_tail(head, rest):
    shapes = ((OWN, W, W), (OWN, W - HALF, W))
    return pl.pallas_call(
        factor_tail_kernel,
        out_shape=tuple(jax.ShapeDtypeStruct(x, F32) for x in shapes),
        in_specs=[VMEM] * 2,
        out_specs=(VMEM,) * 2,
        scratch_shapes=[pltpu.VMEM(rest.shape, F32)],
        compiler_params=PARAMS,
        name="factor_tail",
    )(head, rest)


def split_kernel(r_ref, panel_ref, *refs):
    first, second, sems = refs[:ROWS], refs[ROWS : ROWS + 4], refs[-1]
    r = r_ref[0]
    copies = []
    for s in range(ROWS):
        source = panel_ref.at[pl.ds(lax.rem(r + s, ROWS) * OWN, OWN), :, :HALF]
        copies.append(pltpu.make_async_copy(source, first[s], sems.at[s]))
    for s in range(4):
        source = panel_ref.at[pl.ds(lax.rem(r // 2 + s, 4) * 2 * OWN, 2 * OWN), :, HALF:]
        copies.append(pltpu.make_async_copy(source, second[s], sems.at[ROWS + s]))
    for c in copies:
        c.start()
    for c in copies:
        c.wait()


def split(r, panel):
    piece = jax.ShapeDtypeStruct((OWN, PART, HALF), panel.dtype)
    pair = jax.ShapeDtypeStruct((2 * OWN, PART, HALF), panel.dtype)
    outs = pl.pallas_call(
        split_kernel,
        out_shape=(piece,) * ROWS + (pair,) * 4,
        in_specs=[SMEM, ANY],
        out_specs=(VMEM,) * (ROWS + 4),
        scratch_shapes=[pltpu.SemaphoreType.DMA((ROWS + 4,))],
        compiler_params=PARAMS,
        name="split",
    )(r, panel)
    return outs[:ROWS], outs[ROWS:]


def partner_kernel(r_ref, *refs):
    at = pl.ds((1 - lax.rem(r_ref[0], 2)) * OWN, OWN)
    for s in range(4):
        refs[4][s] = refs[s][at]


def partners(r, pairs):
    return pl.pallas_call(
        partner_kernel,
        out_shape=jax.ShapeDtypeStruct((4, OWN, PART, HALF), F32),
        in_specs=[SMEM] + [VMEM] * 4,
        out_specs=VMEM,
        compiler_params=PARAMS,
        name="partners",
    )(r, *keep(pairs))


def join_kernel(r_ref, *refs):
    pieces, out_ref, sems = refs[:ROWS], refs[ROWS], refs[ROWS + 1]
    copies = []
    for s in range(ROWS):
        source = lax.rem(r_ref[0] + ROWS - s, ROWS)
        copies.append(
            pltpu.make_async_copy(pieces[s], out_ref.at[pl.ds(source * OWN, OWN)], sems.at[s])
        )
    for c in copies:
        c.start()
    for c in copies:
        c.wait()


def join(r, pieces):
    return pl.pallas_call(
        join_kernel,
        out_shape=jax.ShapeDtypeStruct((K,) + pieces[0].shape[1:], pieces[0].dtype),
        in_specs=[SMEM] + [ANY] * ROWS,
        out_specs=VMEM,
        scratch_shapes=[pltpu.SemaphoreType.DMA((ROWS,))],
        compiler_params=PARAMS,
        name="join",
    )(r, *pieces)


def solve_kernel(halves, r_ref, v_ref, *refs):
    n = ROWS + 5 * (halves - 1)
    first, second, outs = refs[:ROWS], refs[ROWS:n], refs[n : n + ROWS]
    t_ref, p_ref = refs[n + ROWS :]
    r = r_ref[0]
    y, core = r // 2, lax.rem(r, 2)

    def rows(source):
        return pl.ds(pl.multiple_of(source * PART, PART), PART)

    for s in range(ROWS):
        p_ref[:, rows(lax.rem(r + ROWS - s, ROWS)), :HALF] = first[s][...]
    for s in range(4 if halves == 2 else 0):
        chip = 2 * lax.rem(y + 4 - s, 4)
        p_ref[:, rows(chip + core), HALF:] = second[s][pl.ds(core * OWN, OWN)]
        p_ref[:, rows(chip + 1 - core), HALF:] = second[4][s]
    for m in range(OWN):
        t_ref[m] = mm_turned(v_ref[m], p_ref[m]).astype(BF16)
    for s in range(ROWS):
        to = lax.rem(r + s, ROWS)
        outs[s][...] = t_ref[:, pl.ds(pl.multiple_of(to * SLICE, SLICE), SLICE), :]


def solve(r, inverse, first, second=()):
    halves = 2 if second else 1
    piece = jax.ShapeDtypeStruct((OWN, SLICE, PANEL), BF16)
    *outs, turned = pl.pallas_call(
        functools.partial(solve_kernel, halves),
        out_shape=(piece,) * ROWS + (jax.ShapeDtypeStruct((OWN, HALF, PANEL), BF16),),
        in_specs=[SMEM] + [VMEM] * (1 + ROWS + len(second)),
        out_specs=(VMEM,) * (ROWS + 1),
        scratch_shapes=[pltpu.VMEM((OWN, PANEL, halves * HALF), F32)],
        compiler_params=PARAMS,
        name="solve",
    )(r, inverse, *keep(first), *keep(second))
    return outs, turned


def turn_kernel(r_ref, a_ref, b_ref, *refs):
    outs, x_ref = refs[:ROWS], refs[ROWS]
    for m in range(OWN):
        x_ref[m, :, :HALF] = a_ref[m].T
        x_ref[m, :, HALF:] = b_ref[m].T
    for s in range(ROWS):
        to = lax.rem(r_ref[0] + s, ROWS)
        outs[s][...] = x_ref[:, pl.ds(pl.multiple_of(to * PART, PART), PART), :]


def turn(r, a, b):
    return pl.pallas_call(
        turn_kernel,
        out_shape=(jax.ShapeDtypeStruct((OWN, PART, W), BF16),) * ROWS,
        in_specs=[SMEM, VMEM, VMEM],
        out_specs=(VMEM,) * ROWS,
        scratch_shapes=[pltpu.VMEM((OWN, PANEL, W), BF16)],
        compiler_params=PARAMS,
        name="turn",
    )(r, a, b)


def outgoing_kernel(r_ref, owner_ref, *refs):
    pieces, out_ref = refs[:ROWS], refs[ROWS]
    used, place = refs[ROWS + 1 :]
    for a in range(LEAVES):
        used[a] = 0
    for k in range(K):
        a = owner_ref[k]
        place[k] = MOST * a + used[a]
        used[a] = used[a] + 1
    for s in range(ROWS):
        source = lax.rem(r_ref[0] + ROWS - s, ROWS)
        for i in range(OWN):
            out_ref[place[source * OWN + i]] = pieces[s][i]


def outgoing(r, owners, pieces):
    return pl.pallas_call(
        outgoing_kernel,
        out_shape=pltpu.VMEM((SLOTS, SLICE, PANEL), BF16),
        in_specs=[SMEM, SMEM] + [VMEM] * ROWS,
        out_specs=VMEM,
        scratch_shapes=[pltpu.SMEM((LEAVES,), jnp.int32), pltpu.SMEM((K,), jnp.int32)],
        compiler_params=PARAMS,
        name="outgoing",
    )(r, owners, *keep(pieces))


def children_kernel(leaf_ref, owner_ref, rel_ref, out_ref):
    me = leaf_ref[0]
    node = lax.broadcasted_iota(jnp.int32, (LEAVES, K), 1)
    hit = owner_ref[...] == me
    first = jnp.min(jnp.where(hit, node, K), axis=1, keepdims=True)
    second = jnp.max(jnp.where(hit, node, -1), axis=1, keepdims=True)
    filled = ((first < K).astype(jnp.int32), (second > first).astype(jnp.int32))
    entry = lax.broadcasted_iota(jnp.int32, (LEAVES, K * P_SIZE), 1)
    lane = lax.broadcasted_iota(jnp.int32, (LEAVES, 128), 1)
    f = rel_ref[...]
    place = lax.rem(f, 2) * 4 + f // 2
    out = jnp.zeros((LEAVES, 128), jnp.int32)
    for s, at in enumerate((first, second)):
        out = jnp.where(lane == s, filled[s], out)
        for p in range(P_SIZE):
            block = jnp.sum(jnp.where(entry == at * P_SIZE + p, place, 0), axis=1, keepdims=True)
            out = jnp.where(lane == MOST + s * P_SIZE + p, block, out)
    out_ref[...] = out


def children(leaf, owners, rel):
    return pl.pallas_call(
        children_kernel,
        out_shape=jax.ShapeDtypeStruct((LEAVES, 128), jnp.int32),
        in_specs=[SMEM, VMEM, VMEM],
        out_specs=VMEM,
        name="children",
    )(leaf, owners, rel)


GROUP = 8
DEPTH = 2 * SLICE


def product_kernel(last, r_ref, table_ref, a_ref, b_ref, *refs):
    z_ref, slot_ref = refs[-2:]
    if last:
        before_ref, outs, acc_ref = refs[0], refs[1:5], refs[5]
    else:
        acc_ref = refs[0]
    y, core = r_ref[0] // 2, lax.rem(r_ref[0], 2)

    def from_leaf(j, count):
        for s in range(MOST):
            filled = table_ref[j, s]

            @pl.when(filled == 1)
            def _():
                slot_ref[count] = MOST * j + s

            count = count + filled
        return count

    count = lax.fori_loop(0, LEAVES, from_leaf, 0)
    acc_ref[...] = before_ref[...] if last else jnp.zeros_like(acc_ref)
    groups = (count + GROUP - 1) // GROUP

    @pl.loop(0, groups)
    def _(g):
        z_ref[...] = jnp.zeros_like(z_ref)
        for i in range(GROUP):
            n = g * GROUP + i

            @pl.when(n < count)
            def _():
                slot = slot_ref[n]
                for p in range(P_SIZE):
                    at = table_ref[slot // MOST, MOST + lax.rem(slot, MOST) * P_SIZE + p]
                    to = pl.ds(pl.multiple_of(at * BS, BS), BS)
                    for h, from_ref in enumerate((a_ref, b_ref)):
                        rows = slice(i * DEPTH + h * SLICE, i * DEPTH + (h + 1) * SLICE)
                        z_ref[rows, to] = from_ref[slot, :, p * BS : (p + 1) * BS]

        half = z_ref[:, pl.ds(pl.multiple_of(core * 4 * BS, 4 * BS), 4 * BS)]
        acc_ref[...] += lax.dot_general(
            half, z_ref[...], (((0,), (0,)), ((), ())), preferred_element_type=F32
        )

    if last:
        for s in range(4):
            x = acc_ref[pl.ds(pl.multiple_of(lax.rem(y + s, 4) * BS, BS), BS), :]
            if s == 0:
                outs[s][...] = x
                continue
            most = jnp.max(jnp.abs(x), axis=0, keepdims=True)
            power = jnp.ceil(jnp.log2(jnp.maximum(most, 1e-30)) - 14.998)
            outs[s][:BS, :] = to_i16(jnp.floor(x * jnp.exp2(-power) + 0.5))
            outs[s][BS:, :] = to_i16(jnp.broadcast_to(power, (16, FB * BS)))


def to_i16(x):
    return x.astype(jnp.int32).astype(jnp.int16)


def product(r, table, a, b, before=None):
    last = before is not None
    a, b = keep((a, b))
    total = (4 * BS, FB * BS)
    own = jax.ShapeDtypeStruct((BS, FB * BS), F32)
    coded = jax.ShapeDtypeStruct((BS + 16, FB * BS), jnp.int16)
    return pl.pallas_call(
        functools.partial(product_kernel, last),
        out_shape=(own, coded, coded, coded) if last else jax.ShapeDtypeStruct(total, F32),
        in_specs=[SMEM] * 2 + [VMEM, VMEM] + ([VMEM] if last else []),
        out_specs=(VMEM,) * 4 if last else VMEM,
        scratch_shapes=([pltpu.VMEM(total, F32)] if last else [])
        + [
            pltpu.VMEM((GROUP * DEPTH, FB * BS), BF16),
            pltpu.SMEM((SLOTS,), jnp.int32),
        ],
        compiler_params=PARAMS,
        name="product",
    )(r, table, a, b, *([before] if last else []))


def subtract_kernel(front_ref, own_ref, *refs):
    parts, out_ref = refs[:3], refs[3]
    for place in range(FB):
        at = slice(place * BS, (place + 1) * BS)
        total = own_ref[:, at]
        for part in parts:
            scale = jnp.exp2(part[BS:, at].astype(jnp.int32).astype(F32)[:1])
            total = total + part[:BS, at].astype(jnp.int32).astype(F32) * scale
        f = 2 * (place % 4) + place // 4
        rows = slice(f * BS, (f + 1) * BS)
        out_ref[rows, :] = front_ref[rows, :] - total.T


def subtract(front, own, parts):
    return pl.pallas_call(
        subtract_kernel,
        out_shape=jax.ShapeDtypeStruct(front.shape, F32),
        in_specs=[VMEM] * 5,
        out_specs=VMEM,
        compiler_params=PARAMS,
        name="subtract",
    )(front, own, *parts)


def shift_row(x, s):
    return lax.ppermute(x, "row", [(i, (i + s) % ROWS) for i in range(ROWS)])


def shift_y(x, s):
    return lax.ppermute(x, "row", [(i, (i + 2 * s) % ROWS) for i in range(ROWS)])


def swap_core(x):
    return lax.ppermute(x, "row", [(i, i ^ 1) for i in range(ROWS)])


def over_row(pieces):
    return [pieces[0]] + [shift_row(pieces[s], s) for s in range(1, ROWS)]


def to_parents(sent):
    sent = sent.reshape(LEAVES, MOST, SLICE, PANEL)
    received = lax.all_to_all(sent, "leaf", split_axis=0, concat_axis=0, tiled=True)
    return received.reshape(SLOTS, SLICE, PANEL)


def on_device(diag_blocks, panel, parent, rel, front):
    r = lax.axis_index("row").reshape(1)
    leaf = lax.axis_index("leaf").reshape(1)
    owners = parent.reshape(LEAVES * K)
    my_owners = lax.dynamic_slice(owners, (leaf[0] * K,), (K,))
    first, second = split(r, panel[0])
    first = over_row(first)
    head, inverse, rest = factor_head(diag_blocks[0])
    outs, turned = solve(r, inverse, first)
    sent = outgoing(r, my_owners, over_row(outs))
    sent, head, rest, second = lax.optimization_barrier((sent, head, rest, second))
    second = [second[0]] + [shift_y(second[s], s) for s in range(1, 4)]
    received = to_parents(sent)
    factors, inverse = factor_tail(head, rest)
    second, inverse = lax.optimization_barrier((second, inverse))
    second.append(swap_core(partners(r, second)))
    outs, turned_too = solve(r, inverse, first, second)
    sent = outgoing(r, my_owners, over_row(outs))
    received, sent, turned, turned_too, parent, rel = lax.optimization_barrier(
        (received, sent, turned, turned_too, parent, rel)
    )
    received_too = to_parents(sent)
    table = children(leaf, parent.reshape(LEAVES, K), rel.reshape(LEAVES, K * P_SIZE))
    total = product(r, table, received, swap_core(received))
    factor_panel = join(r, over_row(turn(r, turned, turned_too)))
    received_too, total, factor_panel = lax.optimization_barrier((received_too, total, factor_panel))
    sums = product(r, table, received_too, swap_core(received_too), total)
    new_front = subtract(front[0], sums[0], [shift_y(sums[s], s) for s in range(1, 4)])
    return (factors[None], factor_panel[None], new_front[None])


def solution(mesh):
    in_specs = (
        P("leaf", "row", None, None),
        P("leaf", None, "row", None),
        P(),
        P(),
        P("leaf", None, "row"),
    )
    out_specs = (P("leaf", "row", None, None), P("leaf", None, "row", None), P("leaf", None, "row"))
    return jax.shard_map(
        on_device, mesh=mesh, in_specs=in_specs, out_specs=out_specs, check_vma=False
    )
```

```python
import functools

import jax
import jax.numpy as jnp
from jax import lax
from jax.experimental import pallas as pl
from jax.experimental.pallas import tpu as pltpu
from jax.sharding import PartitionSpec as P

W = 256
BS = 128
FB = 8
P_SIZE = 6
K = 24
LEAVES = 32
ROWS = 8
OWN = K // ROWS
PANEL = P_SIZE * BS
PART = PANEL // ROWS
HALF = W // 2
SLICE = HALF // ROWS
MOST = 2
SLOTS = LEAVES * MOST
NB = 64
HI = lax.Precision.HIGHEST
F32 = jnp.float32
BF16 = jnp.bfloat16

ANY = pl.BlockSpec(memory_space=pl.ANY)
VMEM = pl.BlockSpec(memory_space=pltpu.VMEM)
SMEM = pl.BlockSpec(memory_space=pltpu.SMEM)
PARAMS = pltpu.CompilerParams(vmem_limit_bytes=32 * 2**20)


def keep(arrays):
    return [pltpu.with_memory_space_constraint(x, pltpu.VMEM) for x in arrays]


def mm(a, b):
    return lax.dot_general(a, b, (((1,), (0,)), ((), ())), precision=HI, preferred_element_type=F32)


def two_parts(x):
    high = x.astype(BF16)
    return high, (x - high.astype(F32)).astype(BF16)


def mm_turned(a, b):
    dot = lambda x, y: lax.dot_general(x, y, (((1,), (1,)), ((), ())), preferred_element_type=F32)
    (ah, al), (bh, bl) = two_parts(a), two_parts(b)
    return dot(ah, bh) + (dot(ah, bl) + dot(al, bh))


def lanes(x, at):
    return jnp.broadcast_to(x[:, at : at + 1], (8, 128))


def sublanes(x, at):
    return jnp.broadcast_to(x[at : at + 1, :], (8, 128))


def eliminate(tiles, offset, nb):
    sub = lax.broadcasted_iota(jnp.int32, (8, 128), 0)
    for g in range(nb // 8):
        at = offset + 8 * g
        rows = [[sublanes(ts[g], i) for i in range(8)] for ts in tiles]
        pivots = []
        for ts in tiles:
            cols = [lanes(ts[g], at + j) for j in range(8)]
            pivots.append([[sublanes(cols[j], i) for j in range(i + 1)] for i in range(8)])
        for ts, t, p in zip(tiles, rows, pivots):
            f, inv = [[None] * 8 for _ in range(8)], []
            for j in range(8):
                inv.append(1.0 / p[j][j])
                for i in range(j + 1, 8):
                    f[i][j] = p[i][j] * inv[j]
                for i in range(j + 1, 8):
                    for k in range(j + 1, i + 1):
                        p[i][k] = p[i][k] - f[i][j] * p[k][j]
                    t[i] = t[i] - f[i][j] * t[j]
            w = [t[i] * inv[i] for i in range(8)]
            for i in range(7, -1, -1):
                for j in range(i):
                    w[j] = w[j] - f[i][j] * w[i]
            done = t[0]
            for i in range(1, 8):
                done = jnp.where(sub == i, t[i], done)
            ts[g] = done
            for below in range(g + 1, nb // 8):
                new = ts[below]
                for i in range(8):
                    new = new - lanes(ts[below], at + i) * w[i]
                ts[below] = new
    return tiles


def factor_steps(first, last, s_ref, l_ref, v_ref, base):
    n, w = s_ref.shape[0], s_ref.shape[2]
    lane = lax.broadcasted_iota(jnp.int32, (NB, 128), 1)
    sub = lax.broadcasted_iota(jnp.int32, (NB, 128), 0)
    for k in range(first, last):
        lo, hi = k * NB, (k + 1) * NB
        here = slice(lo - base, hi - base)
        off = lo % 128
        other = NB - off
        tile = slice(lo - off, lo - off + 128)
        own = (lane >= off) & (lane < off + NB)
        eye = (lane - other == sub).astype(F32)
        tiles = []
        for m in range(n):
            b = jnp.where(own, s_ref[m, here, tile], eye)
            tiles.append([b[8 * t : 8 * t + 8] for t in range(NB // 8)])
        tiles = eliminate(tiles, off, NB)
        for m in range(n):
            b = jnp.concatenate(tiles[m], axis=0)
            d = jnp.sum(jnp.where(lane - off == sub, b, 0.0), axis=1, keepdims=True)
            b = b * (1.0 / jnp.sqrt(d))
            up, inv = b[:, off : off + NB], b[:, other : other + NB]
            up = jnp.where(lane[:, :NB] >= sub[:, :NB], up, 0.0)
            inv = jnp.where(lane[:, :NB] <= sub[:, :NB], inv, 0.0)
            g = mm(inv, s_ref[m, here, :])
            left = [g[:, :lo]] if k else []
            right = [g[:, hi:]] if hi < w else []
            r = jnp.concatenate(left + [inv] + right, axis=1)
            col = lax.broadcasted_iota(jnp.int32, (NB, w), 1)
            v_ref[m, lo - first * NB : hi - first * NB, :] = jnp.where(col < hi, r, 0.0)[:, : v_ref.shape[2]]
            zero = [jnp.zeros((NB, lo), F32)] if k else []
            ut = jnp.concatenate(zero + [up] + right, axis=1).T
            l_ref[m, :, lo:hi] = ut
            if hi < w:
                rest = s_ref[m, hi - base :, :]
                at = lax.broadcasted_iota(jnp.int32, rest.shape, 1)
                rest = jnp.where((at >= lo) & (at < hi), 0.0, rest)
                s_ref[m, hi - base :, :] = rest - mm(ut[hi:, :], r)


def factor_head_kernel(a_ref, l_ref, v_ref, rest_ref, s_ref):
    s_ref[...] = a_ref[...]
    factor_steps(0, HALF // NB, s_ref, l_ref, v_ref, 0)
    rest_ref[...] = s_ref[:, HALF:, :]


def factor_tail_kernel(head_ref, rest_ref, l_ref, v_ref, s_ref):
    s_ref[...] = rest_ref[...]
    l_ref[:, :, :HALF] = head_ref[...]
    factor_steps(HALF // NB, W // NB, s_ref, l_ref, v_ref, HALF)


def factor_head(a):
    shapes = ((OWN, W, HALF), (OWN, HALF, HALF))
    return pl.pallas_call(
        factor_head_kernel,
        out_shape=tuple(jax.ShapeDtypeStruct(x, F32) for x in shapes) + (pltpu.HBM((OWN, W - HALF, W), F32),),
        in_specs=[VMEM],
        out_specs=(VMEM,) * 3,
        scratch_shapes=[pltpu.VMEM(a.shape, F32)],
        compiler_params=PARAMS,
        name="factor_head",
    )(a)


def factor_tail(head, rest):
    shapes = ((OWN, W, W), (OWN, W - HALF, W))
    return pl.pallas_call(
        factor_tail_kernel,
        out_shape=tuple(jax.ShapeDtypeStruct(x, F32) for x in shapes),
        in_specs=[VMEM] * 2,
        out_specs=(VMEM,) * 2,
        scratch_shapes=[pltpu.VMEM(rest.shape, F32)],
        compiler_params=PARAMS,
        name="factor_tail",
    )(head, rest)


def split_kernel(pairs, r_ref, panel_ref, *refs):
    outs, sems = refs[:-1], refs[-1]
    r = r_ref[0]
    copies = []
    for s, out in enumerate(outs):
        at = lax.rem(r // 2 + s, 4) * 2 if pairs else lax.rem(r + s, ROWS)
        columns = slice(HALF, W) if pairs else slice(0, HALF)
        source = panel_ref.at[pl.ds(at * OWN, out.shape[0]), :, columns]
        copies.append(pltpu.make_async_copy(source, out, sems.at[s]))
    for c in copies:
        c.start()
    for c in copies:
        c.wait()


def split(r, panel, pairs):
    n = 4 if pairs else ROWS
    piece = jax.ShapeDtypeStruct((K // n, PART, HALF), panel.dtype)
    return pl.pallas_call(
        functools.partial(split_kernel, pairs),
        out_shape=(piece,) * n,
        in_specs=[SMEM, ANY],
        out_specs=(VMEM,) * n,
        scratch_shapes=[pltpu.SemaphoreType.DMA((n,))],
        compiler_params=PARAMS,
        name="split",
    )(r, panel)


def partner_kernel(r_ref, *refs):
    at = pl.ds((1 - lax.rem(r_ref[0], 2)) * OWN, OWN)
    for s in range(4):
        refs[4][s] = refs[s][at]


def partners(r, pairs):
    return pl.pallas_call(
        partner_kernel,
        out_shape=jax.ShapeDtypeStruct((4, OWN, PART, HALF), F32),
        in_specs=[SMEM] + [VMEM] * 4,
        out_specs=VMEM,
        compiler_params=PARAMS,
        name="partners",
    )(r, *keep(pairs))


def join_kernel(r_ref, *refs):
    pieces, out_ref, sems = refs[:ROWS], refs[ROWS], refs[ROWS + 1]
    copies = []
    for s in range(ROWS):
        source = lax.rem(r_ref[0] + ROWS - s, ROWS)
        copies.append(
            pltpu.make_async_copy(pieces[s], out_ref.at[pl.ds(source * OWN, OWN)], sems.at[s])
        )
    for c in copies:
        c.start()
    for c in copies:
        c.wait()


def join(r, pieces):
    return pl.pallas_call(
        join_kernel,
        out_shape=jax.ShapeDtypeStruct((K,) + pieces[0].shape[1:], pieces[0].dtype),
        in_specs=[SMEM] + [ANY] * ROWS,
        out_specs=VMEM,
        scratch_shapes=[pltpu.SemaphoreType.DMA((ROWS,))],
        compiler_params=PARAMS,
        name="join",
    )(r, *pieces)


def solve_kernel(halves, r_ref, v_ref, *refs):
    n = ROWS + 5 * (halves - 1)
    first, second, outs = refs[:ROWS], refs[ROWS:n], refs[n : n + ROWS]
    t_ref, p_ref = refs[n + ROWS :]
    r = r_ref[0]
    y, core = r // 2, lax.rem(r, 2)

    def rows(source):
        return pl.ds(pl.multiple_of(source * PART, PART), PART)

    for s in range(ROWS):
        p_ref[:, rows(lax.rem(r + ROWS - s, ROWS)), :HALF] = first[s][...]
    for s in range(4 if halves == 2 else 0):
        chip = 2 * lax.rem(y + 4 - s, 4)
        p_ref[:, rows(chip + core), HALF:] = second[s][pl.ds(core * OWN, OWN)]
        p_ref[:, rows(chip + 1 - core), HALF:] = second[4][s]
    for m in range(OWN):
        t_ref[m] = mm_turned(v_ref[m], p_ref[m]).astype(BF16)
    for s in range(ROWS):
        to = lax.rem(r + s, ROWS)
        outs[s][...] = t_ref[:, pl.ds(pl.multiple_of(to * SLICE, SLICE), SLICE), :]


def solve(r, inverse, first, second=()):
    halves = 2 if second else 1
    piece = jax.ShapeDtypeStruct((OWN, SLICE, PANEL), BF16)
    *outs, turned = pl.pallas_call(
        functools.partial(solve_kernel, halves),
        out_shape=(piece,) * ROWS + (pltpu.HBM((OWN, HALF, PANEL), BF16),),
        in_specs=[SMEM] + [VMEM] * (1 + ROWS + len(second)),
        out_specs=(VMEM,) * (ROWS + 1),
        scratch_shapes=[pltpu.VMEM((OWN, PANEL, halves * HALF), F32)],
        compiler_params=PARAMS,
        name="solve",
    )(r, inverse, *keep(first), *keep(second))
    return outs, turned


def turn_kernel(r_ref, a_ref, b_ref, *refs):
    outs, x_ref = refs[:ROWS], refs[ROWS]
    for m in range(OWN):
        x_ref[m, :, :HALF] = a_ref[m].T
        x_ref[m, :, HALF:] = b_ref[m].T
    for s in range(ROWS):
        to = lax.rem(r_ref[0] + s, ROWS)
        outs[s][...] = x_ref[:, pl.ds(pl.multiple_of(to * PART, PART), PART), :]


def turn(r, a, b):
    return pl.pallas_call(
        turn_kernel,
        out_shape=(jax.ShapeDtypeStruct((OWN, PART, W), BF16),) * ROWS,
        in_specs=[SMEM, VMEM, VMEM],
        out_specs=(VMEM,) * ROWS,
        scratch_shapes=[pltpu.VMEM((OWN, PANEL, W), BF16)],
        compiler_params=PARAMS,
        name="turn",
    )(r, a, b)


def outgoing_kernel(r_ref, owner_ref, *refs):
    pieces, out_ref = refs[:ROWS], refs[ROWS]
    used, place = refs[ROWS + 1 :]
    for a in range(LEAVES):
        used[a] = 0
    for k in range(K):
        a = owner_ref[k]
        place[k] = MOST * a + used[a]
        used[a] = used[a] + 1
    for s in range(ROWS):
        source = lax.rem(r_ref[0] + ROWS - s, ROWS)
        for i in range(OWN):
            out_ref[place[source * OWN + i]] = pieces[s][i]


def outgoing(r, owners, pieces):
    return pl.pallas_call(
        outgoing_kernel,
        out_shape=pltpu.VMEM((SLOTS, SLICE, PANEL), BF16),
        in_specs=[SMEM, SMEM] + [VMEM] * ROWS,
        out_specs=VMEM,
        scratch_shapes=[pltpu.SMEM((LEAVES,), jnp.int32), pltpu.SMEM((K,), jnp.int32)],
        compiler_params=PARAMS,
        name="outgoing",
    )(r, owners, *keep(pieces))


def children_kernel(leaf_ref, owner_ref, rel_ref, out_ref):
    me = leaf_ref[0]
    node = lax.broadcasted_iota(jnp.int32, (LEAVES, K), 1)
    hit = owner_ref[...] == me
    first = jnp.min(jnp.where(hit, node, K), axis=1, keepdims=True)
    second = jnp.max(jnp.where(hit, node, -1), axis=1, keepdims=True)
    filled = ((first < K).astype(jnp.int32), (second > first).astype(jnp.int32))
    entry = lax.broadcasted_iota(jnp.int32, (LEAVES, K * P_SIZE), 1)
    lane = lax.broadcasted_iota(jnp.int32, (LEAVES, 128), 1)
    f = rel_ref[...]
    place = lax.rem(f, 2) * 4 + f // 2
    out = jnp.zeros((LEAVES, 128), jnp.int32)
    for s, at in enumerate((first, second)):
        out = jnp.where(lane == s, filled[s], out)
        for p in range(P_SIZE):
            block = jnp.sum(jnp.where(entry == at * P_SIZE + p, place, 0), axis=1, keepdims=True)
            out = jnp.where(lane == MOST + s * P_SIZE + p, block, out)
    out_ref[...] = out


def children(leaf, owners, rel):
    return pl.pallas_call(
        children_kernel,
        out_shape=jax.ShapeDtypeStruct((LEAVES, 128), jnp.int32),
        in_specs=[SMEM, VMEM, VMEM],
        out_specs=VMEM,
        name="children",
    )(leaf, owners, rel)


GROUP = 16
DEPTH = 2 * SLICE


def product_kernel(shifts, r_ref, table_ref, a_ref, b_ref, *refs):
    last = shifts is not None
    z_ref, slot_ref = refs[-2:]
    if last:
        before_ref, outs, acc_ref = refs[0], refs[1:-3], refs[-3]
    else:
        acc_ref = refs[0]
    y, core = r_ref[0] // 2, lax.rem(r_ref[0], 2)

    def from_leaf(j, count):
        for s in range(MOST):
            filled = table_ref[j, s]

            @pl.when(filled == 1)
            def _():
                slot_ref[count] = MOST * j + s

            count = count + filled
        return count

    count = lax.fori_loop(0, LEAVES, from_leaf, 0)
    held = [lax.rem(y + s, 4) for s in shifts] if last else list(range(4))
    for i, at in enumerate(held):
        rows = slice(i * BS, (i + 1) * BS)
        if last:
            acc_ref[rows, :] = before_ref[pl.ds(pl.multiple_of(at * BS, BS), BS), :]
        else:
            acc_ref[rows, :] = jnp.zeros((BS, FB * BS), F32)
    groups = (count + GROUP - 1) // GROUP

    @pl.loop(0, groups)
    def _(g):
        z_ref[...] = jnp.zeros_like(z_ref)
        for i in range(GROUP):
            n = g * GROUP + i

            @pl.when(n < count)
            def _():
                slot = slot_ref[n]
                for p in range(P_SIZE):
                    at = table_ref[slot // MOST, MOST + lax.rem(slot, MOST) * P_SIZE + p]
                    to = pl.ds(pl.multiple_of(at * BS, BS), BS)
                    for h, from_ref in enumerate((a_ref, b_ref)):
                        rows = slice(i * DEPTH + h * SLICE, i * DEPTH + (h + 1) * SLICE)
                        z_ref[rows, to] = from_ref[slot, :, p * BS : (p + 1) * BS]

        parts = [z_ref[:, pl.ds(pl.multiple_of((core * 4 + at) * BS, BS), BS)] for at in held]
        acc_ref[...] += lax.dot_general(
            jnp.concatenate(parts, axis=1), z_ref[...], (((0,), (0,)), ((), ())), preferred_element_type=F32
        )

    for i, s in enumerate(shifts if last else ()):
        x = acc_ref[i * BS : (i + 1) * BS, :]
        if s == 0:
            outs[i][...] = x
            continue
        most = jnp.max(jnp.abs(x), axis=0, keepdims=True)
        power = jnp.ceil(jnp.log2(jnp.maximum(most, 1e-30)) - 14.998)
        outs[i][:BS, :] = to_i16(jnp.floor(x * jnp.exp2(-power) + 0.5))
        outs[i][BS:, :] = to_i16(jnp.broadcast_to(power, (16, FB * BS)))


def to_i16(x):
    return x.astype(jnp.int32).astype(jnp.int16)


def product(r, table, a, b, before=None, shifts=None):
    last = before is not None
    a, b = keep((a, b))
    total = jax.ShapeDtypeStruct((4 * BS, FB * BS), F32)
    own = jax.ShapeDtypeStruct((BS, FB * BS), F32)
    coded = jax.ShapeDtypeStruct((BS + 16, FB * BS), jnp.int16)
    outs = [coded if s else own for s in shifts] if last else [total]
    return pl.pallas_call(
        functools.partial(product_kernel, shifts),
        out_shape=outs if last else total,
        in_specs=[SMEM] * 2 + [VMEM, VMEM] + ([VMEM] if last else []),
        out_specs=[VMEM] * len(outs) if last else VMEM,
        scratch_shapes=([pltpu.VMEM((len(outs) * BS, FB * BS), F32)] if last else [])
        + [
            pltpu.VMEM((GROUP * DEPTH, FB * BS), BF16),
            pltpu.SMEM((SLOTS,), jnp.int32),
        ],
        compiler_params=PARAMS,
        name="product",
    )(r, table, a, b, *([before] if last else []))


def subtract_kernel(front_ref, own_ref, *refs):
    parts, out_ref = refs[:3], refs[3]
    for place in range(FB):
        at = slice(place * BS, (place + 1) * BS)
        total = own_ref[:, at]
        for part in parts:
            scale = jnp.exp2(part[BS:, at].astype(jnp.int32).astype(F32)[:1])
            total = total + part[:BS, at].astype(jnp.int32).astype(F32) * scale
        f = 2 * (place % 4) + place // 4
        rows = slice(f * BS, (f + 1) * BS)
        out_ref[rows, :] = front_ref[rows, :] - total.T


def subtract(front, own, parts):
    return pl.pallas_call(
        subtract_kernel,
        out_shape=jax.ShapeDtypeStruct(front.shape, F32),
        in_specs=[VMEM] * 5,
        out_specs=VMEM,
        compiler_params=PARAMS,
        name="subtract",
    )(front, own, *parts)


def shift_row(x, s):
    return lax.ppermute(x, "row", [(i, (i + s) % ROWS) for i in range(ROWS)])


def shift_y(x, s):
    return lax.ppermute(x, "row", [(i, (i + 2 * s) % ROWS) for i in range(ROWS)])


def swap_core(x):
    return lax.ppermute(x, "row", [(i, i ^ 1) for i in range(ROWS)])


def over_row(pieces):
    return [pieces[0]] + [shift_row(pieces[s], s) for s in range(1, ROWS)]


def to_parents(sent):
    sent = sent.reshape(LEAVES, MOST, SLICE, PANEL)
    received = lax.all_to_all(sent, "leaf", split_axis=0, concat_axis=0, tiled=True)
    return received.reshape(SLOTS, SLICE, PANEL)


def on_device(diag_blocks, panel, parent, rel, front):
    r = lax.axis_index("row").reshape(1)
    leaf = lax.axis_index("leaf").reshape(1)
    owners = parent.reshape(LEAVES * K)
    my_owners = lax.dynamic_slice(owners, (leaf[0] * K,), (K,))
    first = over_row(split(r, panel[0], False))
    head, inverse, rest = factor_head(diag_blocks[0])
    outs, turned = solve(r, inverse, first)
    sent = outgoing(r, my_owners, over_row(outs))
    sent, head, rest, panel = lax.optimization_barrier((sent, head, rest, panel))
    second = split(r, panel[0], True)
    second = [second[0]] + [shift_y(second[s], s) for s in range(1, 4)]
    received = to_parents(sent)
    factors, inverse = factor_tail(head, rest)
    second, inverse = lax.optimization_barrier((second, inverse))
    second.append(swap_core(partners(r, second)))
    outs, turned_too = solve(r, inverse, first, second)
    sent = outgoing(r, my_owners, over_row(outs))
    received, sent, turned, turned_too, parent, rel = lax.optimization_barrier(
        (received, sent, turned, turned_too, parent, rel)
    )
    received_too = to_parents(sent)
    table = children(leaf, parent.reshape(LEAVES, K), rel.reshape(LEAVES, K * P_SIZE))
    total = product(r, table, received, swap_core(received))
    by_row = over_row(turn(r, turned, turned_too))
    received_too, total, by_row = lax.optimization_barrier((received_too, total, by_row))
    factor_panel = join(r, by_row)
    swapped = swap_core(received_too)
    two, one = product(r, table, received_too, swapped, total, (2, 1))
    three, own = product(r, table, received_too, swapped, total, (3, 0))
    parts = [shift_y(x, s) for x, s in ((one, 1), (two, 2), (three, 3))]
    new_front = subtract(front[0], own, parts)
    return (factors[None], factor_panel[None], new_front[None])


def solution(mesh):
    in_specs = (
        P("leaf", "row", None, None),
        P("leaf", None, "row", None),
        P(),
        P(),
        P("leaf", None, "row"),
    )
    out_specs = (P("leaf", "row", None, None), P("leaf", None, "row", None), P("leaf", None, "row"))
    return jax.shard_map(
        on_device, mesh=mesh, in_specs=in_specs, out_specs=out_specs, check_vma=False
    )
```

```python
import functools

import jax
import jax.numpy as jnp
from jax import lax
from jax.experimental import pallas as pl
from jax.experimental.pallas import tpu as pltpu
from jax.sharding import PartitionSpec as P

W = 256
BS = 128
FB = 8
P_SIZE = 6
K = 24
LEAVES = 32
ROWS = 8
OWN = K // ROWS
PANEL = P_SIZE * BS
PART = PANEL // ROWS
HALF = W // 2
SLICE = HALF // ROWS
MOST = 2
SLOTS = LEAVES * MOST
NB = 64
HI = lax.Precision.HIGHEST
F32 = jnp.float32
BF16 = jnp.bfloat16

ANY = pl.BlockSpec(memory_space=pl.ANY)
VMEM = pl.BlockSpec(memory_space=pltpu.VMEM)
SMEM = pl.BlockSpec(memory_space=pltpu.SMEM)
PARAMS = pltpu.CompilerParams(vmem_limit_bytes=32 * 2**20)


def keep(arrays):
    return [pltpu.with_memory_space_constraint(x, pltpu.VMEM) for x in arrays]


def mm(a, b):
    return lax.dot_general(a, b, (((1,), (0,)), ((), ())), precision=HI, preferred_element_type=F32)


def two_parts(x):
    high = x.astype(BF16)
    return high, (x - high.astype(F32)).astype(BF16)


def mm_turned(a, b):
    dot = lambda x, y: lax.dot_general(x, y, (((1,), (1,)), ((), ())), preferred_element_type=F32)
    (ah, al), (bh, bl) = two_parts(a), two_parts(b)
    return dot(ah, bh) + (dot(ah, bl) + dot(al, bh))


def lanes(x, at):
    return jnp.broadcast_to(x[:, at : at + 1], (8, 128))


def sublanes(x, at):
    return jnp.broadcast_to(x[at : at + 1, :], (8, 128))


def eliminate(tiles, offset, nb):
    sub = lax.broadcasted_iota(jnp.int32, (8, 128), 0)
    for g in range(nb // 8):
        at = offset + 8 * g
        rows = [[sublanes(ts[g], i) for i in range(8)] for ts in tiles]
        pivots = []
        for ts in tiles:
            cols = [lanes(ts[g], at + j) for j in range(8)]
            pivots.append([[sublanes(cols[j], i) for j in range(i + 1)] for i in range(8)])
        for ts, t, p in zip(tiles, rows, pivots):
            f, inv = [[None] * 8 for _ in range(8)], []
            for j in range(8):
                inv.append(1.0 / p[j][j])
                for i in range(j + 1, 8):
                    f[i][j] = p[i][j] * inv[j]
                for i in range(j + 1, 8):
                    for k in range(j + 1, i + 1):
                        p[i][k] = p[i][k] - f[i][j] * p[k][j]
                    t[i] = t[i] - f[i][j] * t[j]
            w = [t[i] * inv[i] for i in range(8)]
            for i in range(7, -1, -1):
                for j in range(i):
                    w[j] = w[j] - f[i][j] * w[i]
            done = t[0]
            for i in range(1, 8):
                done = jnp.where(sub == i, t[i], done)
            ts[g] = done
            for below in range(g + 1, nb // 8):
                new = ts[below]
                for i in range(8):
                    new = new - lanes(ts[below], at + i) * w[i]
                ts[below] = new
    return tiles


def factor_steps(first, last, s_ref, l_ref, v_ref, base):
    n, w = s_ref.shape[0], s_ref.shape[2]
    lane = lax.broadcasted_iota(jnp.int32, (NB, 128), 1)
    sub = lax.broadcasted_iota(jnp.int32, (NB, 128), 0)
    for k in range(first, last):
        lo, hi = k * NB, (k + 1) * NB
        here = slice(lo - base, hi - base)
        off = lo % 128
        other = NB - off
        tile = slice(lo - off, lo - off + 128)
        own = (lane >= off) & (lane < off + NB)
        eye = (lane - other == sub).astype(F32)
        tiles = []
        for m in range(n):
            b = jnp.where(own, s_ref[m, here, tile], eye)
            tiles.append([b[8 * t : 8 * t + 8] for t in range(NB // 8)])
        tiles = eliminate(tiles, off, NB)
        for m in range(n):
            b = jnp.concatenate(tiles[m], axis=0)
            d = jnp.sum(jnp.where(lane - off == sub, b, 0.0), axis=1, keepdims=True)
            b = b * (1.0 / jnp.sqrt(d))
            up, inv = b[:, off : off + NB], b[:, other : other + NB]
            up = jnp.where(lane[:, :NB] >= sub[:, :NB], up, 0.0)
            inv = jnp.where(lane[:, :NB] <= sub[:, :NB], inv, 0.0)
            g = mm(inv, s_ref[m, here, :])
            left = [g[:, :lo]] if k else []
            right = [g[:, hi:]] if hi < w else []
            r = jnp.concatenate(left + [inv] + right, axis=1)
            col = lax.broadcasted_iota(jnp.int32, (NB, w), 1)
            v_ref[m, lo - first * NB : hi - first * NB, :] = jnp.where(col < hi, r, 0.0)[:, : v_ref.shape[2]]
            zero = [jnp.zeros((NB, lo), F32)] if k else []
            ut = jnp.concatenate(zero + [up] + right, axis=1).T
            l_ref[m, :, lo:hi] = ut
            if hi < w:
                rest = s_ref[m, hi - base :, :]
                at = lax.broadcasted_iota(jnp.int32, rest.shape, 1)
                rest = jnp.where((at >= lo) & (at < hi), 0.0, rest)
                s_ref[m, hi - base :, :] = rest - mm(ut[hi:, :], r)


def factor_head_kernel(a_ref, l_ref, v_ref, rest_ref, s_ref):
    s_ref[...] = a_ref[...]
    factor_steps(0, HALF // NB, s_ref, l_ref, v_ref, 0)
    rest_ref[...] = s_ref[:, HALF:, :]


def factor_tail_kernel(head_ref, rest_ref, l_ref, v_ref, s_ref):
    s_ref[...] = rest_ref[...]
    l_ref[:, :, :HALF] = head_ref[...]
    factor_steps(HALF // NB, W // NB, s_ref, l_ref, v_ref, HALF)


def factor_head(a):
    shapes = ((OWN, W, HALF), (OWN, HALF, HALF))
    return pl.pallas_call(
        factor_head_kernel,
        out_shape=tuple(jax.ShapeDtypeStruct(x, F32) for x in shapes) + (pltpu.HBM((OWN, W - HALF, W), F32),),
        in_specs=[VMEM],
        out_specs=(VMEM,) * 3,
        scratch_shapes=[pltpu.VMEM(a.shape, F32)],
        compiler_params=PARAMS,
        name="factor_head",
    )(a)


def factor_tail(head, rest):
    shapes = ((OWN, W, W), (OWN, W - HALF, W))
    return pl.pallas_call(
        factor_tail_kernel,
        out_shape=tuple(jax.ShapeDtypeStruct(x, F32) for x in shapes),
        in_specs=[VMEM] * 2,
        out_specs=(VMEM,) * 2,
        scratch_shapes=[pltpu.VMEM(rest.shape, F32)],
        compiler_params=PARAMS,
        name="factor_tail",
    )(head, rest)


def split_kernel(pairs, r_ref, panel_ref, *refs):
    outs, sems = refs[:-1], refs[-1]
    r = r_ref[0]
    copies = []
    for s, out in enumerate(outs):
        at = lax.rem(r // 2 + s, 4) * 2 if pairs else lax.rem(r + s, ROWS)
        columns = slice(HALF, W) if pairs else slice(0, HALF)
        source = panel_ref.at[pl.ds(at * OWN, out.shape[0]), :, columns]
        copies.append(pltpu.make_async_copy(source, out, sems.at[s]))
    for c in copies:
        c.start()
    for c in copies:
        c.wait()


def split(r, panel, pairs):
    n = 4 if pairs else ROWS
    piece = jax.ShapeDtypeStruct((K // n, PART, HALF), panel.dtype)
    return pl.pallas_call(
        functools.partial(split_kernel, pairs),
        out_shape=(piece,) * n,
        in_specs=[SMEM, ANY],
        out_specs=(VMEM,) * n,
        scratch_shapes=[pltpu.SemaphoreType.DMA((n,))],
        compiler_params=PARAMS,
        name="split",
    )(r, pltpu.with_memory_space_constraint(panel, pltpu.HBM))


def partner_kernel(r_ref, *refs):
    at = pl.ds((1 - lax.rem(r_ref[0], 2)) * OWN, OWN)
    for s in range(4):
        refs[4][s] = refs[s][at]


def partners(r, pairs):
    return pl.pallas_call(
        partner_kernel,
        out_shape=jax.ShapeDtypeStruct((4, OWN, PART, HALF), F32),
        in_specs=[SMEM] + [VMEM] * 4,
        out_specs=VMEM,
        compiler_params=PARAMS,
        name="partners",
    )(r, *keep(pairs))


def join_kernel(r_ref, *refs):
    pieces, out_ref, sems = refs[:ROWS], refs[ROWS], refs[ROWS + 1]
    copies = []
    for s in range(ROWS):
        source = lax.rem(r_ref[0] + ROWS - s, ROWS)
        copies.append(
            pltpu.make_async_copy(pieces[s], out_ref.at[pl.ds(source * OWN, OWN)], sems.at[s])
        )
    for c in copies:
        c.start()
    for c in copies:
        c.wait()


def join(r, pieces):
    return pl.pallas_call(
        join_kernel,
        out_shape=jax.ShapeDtypeStruct((K,) + pieces[0].shape[1:], pieces[0].dtype),
        in_specs=[SMEM] + [ANY] * ROWS,
        out_specs=VMEM,
        scratch_shapes=[pltpu.SemaphoreType.DMA((ROWS,))],
        compiler_params=PARAMS,
        name="join",
    )(r, *pieces)


def solve_kernel(halves, r_ref, v_ref, *refs):
    n = ROWS + 5 * (halves - 1)
    first, second, outs = refs[:ROWS], refs[ROWS:n], refs[n : n + ROWS]
    t_ref, p_ref = refs[n + ROWS :]
    r = r_ref[0]
    y, core = r // 2, lax.rem(r, 2)

    def rows(source):
        return pl.ds(pl.multiple_of(source * PART, PART), PART)

    for s in range(ROWS):
        p_ref[:, rows(lax.rem(r + ROWS - s, ROWS)), :HALF] = first[s][...]
    for s in range(4 if halves == 2 else 0):
        chip = 2 * lax.rem(y + 4 - s, 4)
        p_ref[:, rows(chip + core), HALF:] = second[s][pl.ds(core * OWN, OWN)]
        p_ref[:, rows(chip + 1 - core), HALF:] = second[4][s]
    for m in range(OWN):
        t_ref[m] = mm_turned(v_ref[m], p_ref[m]).astype(BF16)
    for s in range(ROWS):
        to = lax.rem(r + s, ROWS)
        outs[s][...] = t_ref[:, pl.ds(pl.multiple_of(to * SLICE, SLICE), SLICE), :]


def solve(r, inverse, first, second=()):
    halves = 2 if second else 1
    piece = jax.ShapeDtypeStruct((OWN, SLICE, PANEL), BF16)
    *outs, turned = pl.pallas_call(
        functools.partial(solve_kernel, halves),
        out_shape=(piece,) * ROWS + (pltpu.HBM((OWN, HALF, PANEL), BF16),),
        in_specs=[SMEM] + [VMEM] * (1 + ROWS + len(second)),
        out_specs=(VMEM,) * (ROWS + 1),
        scratch_shapes=[pltpu.VMEM((OWN, PANEL, halves * HALF), F32)],
        compiler_params=PARAMS,
        name="solve",
    )(r, inverse, *keep(first), *keep(second))
    return outs, turned


def turn_kernel(r_ref, a_ref, b_ref, *refs):
    outs, x_ref = refs[:ROWS], refs[ROWS]
    for m in range(OWN):
        x_ref[m, :, :HALF] = a_ref[m].T
        x_ref[m, :, HALF:] = b_ref[m].T
    for s in range(ROWS):
        to = lax.rem(r_ref[0] + s, ROWS)
        outs[s][...] = x_ref[:, pl.ds(pl.multiple_of(to * PART, PART), PART), :]


def turn(r, a, b):
    return pl.pallas_call(
        turn_kernel,
        out_shape=(jax.ShapeDtypeStruct((OWN, PART, W), BF16),) * ROWS,
        in_specs=[SMEM, VMEM, VMEM],
        out_specs=(VMEM,) * ROWS,
        scratch_shapes=[pltpu.VMEM((OWN, PANEL, W), BF16)],
        compiler_params=PARAMS,
        name="turn",
    )(r, a, b)


def outgoing_kernel(r_ref, owner_ref, *refs):
    pieces, out_ref = refs[:ROWS], refs[ROWS]
    used, place = refs[ROWS + 1 :]
    for a in range(LEAVES):
        used[a] = 0
    for k in range(K):
        a = owner_ref[k]
        place[k] = MOST * a + used[a]
        used[a] = used[a] + 1
    for s in range(ROWS):
        source = lax.rem(r_ref[0] + ROWS - s, ROWS)
        for i in range(OWN):
            out_ref[place[source * OWN + i]] = pieces[s][i]


def outgoing(r, owners, pieces):
    return pl.pallas_call(
        outgoing_kernel,
        out_shape=pltpu.VMEM((SLOTS, SLICE, PANEL), BF16),
        in_specs=[SMEM, SMEM] + [VMEM] * ROWS,
        out_specs=VMEM,
        scratch_shapes=[pltpu.SMEM((LEAVES,), jnp.int32), pltpu.SMEM((K,), jnp.int32)],
        compiler_params=PARAMS,
        name="outgoing",
    )(r, owners, *keep(pieces))


def children_kernel(leaf_ref, owner_ref, rel_ref, out_ref):
    me = leaf_ref[0]
    node = lax.broadcasted_iota(jnp.int32, (LEAVES, K), 1)
    hit = owner_ref[...] == me
    first = jnp.min(jnp.where(hit, node, K), axis=1, keepdims=True)
    second = jnp.max(jnp.where(hit, node, -1), axis=1, keepdims=True)
    filled = ((first < K).astype(jnp.int32), (second > first).astype(jnp.int32))
    entry = lax.broadcasted_iota(jnp.int32, (LEAVES, K * P_SIZE), 1)
    lane = lax.broadcasted_iota(jnp.int32, (LEAVES, 128), 1)
    f = rel_ref[...]
    place = lax.rem(f, 2) * 4 + f // 2
    out = jnp.zeros((LEAVES, 128), jnp.int32)
    for s, at in enumerate((first, second)):
        out = jnp.where(lane == s, filled[s], out)
        for p in range(P_SIZE):
            block = jnp.sum(jnp.where(entry == at * P_SIZE + p, place, 0), axis=1, keepdims=True)
            out = jnp.where(lane == MOST + s * P_SIZE + p, block, out)
    out_ref[...] = out


def children(leaf, owners, rel):
    return pl.pallas_call(
        children_kernel,
        out_shape=jax.ShapeDtypeStruct((LEAVES, 128), jnp.int32),
        in_specs=[SMEM, VMEM, VMEM],
        out_specs=VMEM,
        name="children",
    )(leaf, owners, rel)


GROUP = 16
DEPTH = 2 * SLICE


def product_kernel(shifts, r_ref, table_ref, a_ref, b_ref, *refs):
    last = shifts is not None
    z_ref, slot_ref = refs[-2:]
    if last:
        before_ref, outs, acc_ref = refs[0], refs[1:-3], refs[-3]
    else:
        acc_ref = refs[0]
    y, core = r_ref[0] // 2, lax.rem(r_ref[0], 2)

    def from_leaf(j, count):
        for s in range(MOST):
            filled = table_ref[j, s]

            @pl.when(filled == 1)
            def _():
                slot_ref[count] = MOST * j + s

            count = count + filled
        return count

    count = lax.fori_loop(0, LEAVES, from_leaf, 0)
    held = [lax.rem(y + s, 4) for s in shifts] if last else list(range(4))
    for i, at in enumerate(held):
        rows = slice(i * BS, (i + 1) * BS)
        if last:
            acc_ref[rows, :] = before_ref[pl.ds(pl.multiple_of(at * BS, BS), BS), :]
        else:
            acc_ref[rows, :] = jnp.zeros((BS, FB * BS), F32)
    groups = (count + GROUP - 1) // GROUP

    @pl.loop(0, groups)
    def _(g):
        z_ref[...] = jnp.zeros_like(z_ref)
        for i in range(GROUP):
            n = g * GROUP + i

            @pl.when(n < count)
            def _():
                slot = slot_ref[n]
                for p in range(P_SIZE):
                    at = table_ref[slot // MOST, MOST + lax.rem(slot, MOST) * P_SIZE + p]
                    to = pl.ds(pl.multiple_of(at * BS, BS), BS)
                    for h, from_ref in enumerate((a_ref, b_ref)):
                        rows = slice(i * DEPTH + h * SLICE, i * DEPTH + (h + 1) * SLICE)
                        z_ref[rows, to] = from_ref[slot, :, p * BS : (p + 1) * BS]

        parts = [z_ref[:, pl.ds(pl.multiple_of((core * 4 + at) * BS, BS), BS)] for at in held]
        acc_ref[...] += lax.dot_general(
            jnp.concatenate(parts, axis=1), z_ref[...], (((0,), (0,)), ((), ())), preferred_element_type=F32
        )

    for i, s in enumerate(shifts if last else ()):
        x = acc_ref[i * BS : (i + 1) * BS, :]
        if s == 0:
            outs[i][...] = x
            continue
        most = jnp.max(jnp.abs(x), axis=0, keepdims=True)
        power = jnp.ceil(jnp.log2(jnp.maximum(most, 1e-30)) - 14.998)
        outs[i][:BS, :] = to_i16(jnp.floor(x * jnp.exp2(-power) + 0.5))
        outs[i][BS:, :] = to_i16(jnp.broadcast_to(power, (16, FB * BS)))


def to_i16(x):
    return x.astype(jnp.int32).astype(jnp.int16)


def product(r, table, a, b, before=None, shifts=None):
    last = before is not None
    a, b = keep((a, b))
    total = jax.ShapeDtypeStruct((4 * BS, FB * BS), F32)
    own = jax.ShapeDtypeStruct((BS, FB * BS), F32)
    coded = jax.ShapeDtypeStruct((BS + 16, FB * BS), jnp.int16)
    outs = [coded if s else own for s in shifts] if last else [total]
    return pl.pallas_call(
        functools.partial(product_kernel, shifts),
        out_shape=outs if last else total,
        in_specs=[SMEM] * 2 + [VMEM, VMEM] + ([VMEM] if last else []),
        out_specs=[VMEM] * len(outs) if last else VMEM,
        scratch_shapes=([pltpu.VMEM((len(outs) * BS, FB * BS), F32)] if last else [])
        + [
            pltpu.VMEM((GROUP * DEPTH, FB * BS), BF16),
            pltpu.SMEM((SLOTS,), jnp.int32),
        ],
        compiler_params=PARAMS,
        name="product",
    )(r, table, a, b, *([before] if last else []))


def subtract_kernel(front_ref, own_ref, *refs):
    parts, out_ref = refs[:3], refs[3]
    for place in range(FB):
        at = slice(place * BS, (place + 1) * BS)
        total = own_ref[:, at]
        for part in parts:
            scale = jnp.exp2(part[BS:, at].astype(jnp.int32).astype(F32)[:1])
            total = total + part[:BS, at].astype(jnp.int32).astype(F32) * scale
        f = 2 * (place % 4) + place // 4
        rows = slice(f * BS, (f + 1) * BS)
        out_ref[rows, :] = front_ref[rows, :] - total.T


def subtract(front, own, parts):
    return pl.pallas_call(
        subtract_kernel,
        out_shape=jax.ShapeDtypeStruct(front.shape, F32),
        in_specs=[VMEM] * 5,
        out_specs=VMEM,
        compiler_params=PARAMS,
        name="subtract",
    )(front, own, *parts)


def shift_row(x, s):
    return lax.ppermute(x, "row", [(i, (i + s) % ROWS) for i in range(ROWS)])


def shift_y(x, s):
    return lax.ppermute(x, "row", [(i, (i + 2 * s) % ROWS) for i in range(ROWS)])


def swap_core(x):
    return lax.ppermute(x, "row", [(i, i ^ 1) for i in range(ROWS)])


def over_row(pieces):
    return [pieces[0]] + [shift_row(pieces[s], s) for s in range(1, ROWS)]


def to_parents(sent):
    sent = sent.reshape(LEAVES, MOST, SLICE, PANEL)
    received = lax.all_to_all(sent, "leaf", split_axis=0, concat_axis=0, tiled=True)
    return received.reshape(SLOTS, SLICE, PANEL)


def on_device(diag_blocks, panel, parent, rel, front):
    r = lax.axis_index("row").reshape(1)
    leaf = lax.axis_index("leaf").reshape(1)
    owners = parent.reshape(LEAVES * K)
    my_owners = lax.dynamic_slice(owners, (leaf[0] * K,), (K,))
    first = over_row(split(r, panel[0], False))
    head, inverse, rest = factor_head(diag_blocks[0])
    outs, turned = solve(r, inverse, first)
    sent = outgoing(r, my_owners, over_row(outs))
    sent, head, rest, panel = lax.optimization_barrier((sent, head, rest, panel))
    second = split(r, panel[0], True)
    second = [second[0]] + [shift_y(second[s], s) for s in range(1, 4)]
    received = to_parents(sent)
    factors, inverse = factor_tail(head, rest)
    second, inverse = lax.optimization_barrier((second, inverse))
    second.append(swap_core(partners(r, second)))
    outs, turned_too = solve(r, inverse, first, second)
    sent = outgoing(r, my_owners, over_row(outs))
    received, sent, turned, turned_too, parent, rel = lax.optimization_barrier(
        (received, sent, turned, turned_too, parent, rel)
    )
    received_too = to_parents(sent)
    table = children(leaf, parent.reshape(LEAVES, K), rel.reshape(LEAVES, K * P_SIZE))
    total = product(r, table, received, swap_core(received))
    by_row = over_row(turn(r, turned, turned_too))
    received_too, total, by_row = lax.optimization_barrier((received_too, total, by_row))
    factor_panel = join(r, by_row)
    swapped = swap_core(received_too)
    two, one = product(r, table, received_too, swapped, total, (2, 1))
    three, own = product(r, table, received_too, swapped, total, (3, 0))
    parts = [shift_y(x, s) for x, s in ((one, 1), (two, 2), (three, 3))]
    new_front = subtract(front[0], own, parts)
    return (factors[None], factor_panel[None], new_front[None])


def solution(mesh):
    in_specs = (
        P("leaf", "row", None, None),
        P("leaf", None, "row", None),
        P(),
        P(),
        P("leaf", None, "row"),
    )
    out_specs = (P("leaf", "row", None, None), P("leaf", None, "row", None), P("leaf", None, "row"))
    return jax.shard_map(
        on_device, mesh=mesh, in_specs=in_specs, out_specs=out_specs, check_vma=False
    )
```
